32 devices in a mesh: fsdp: 8 (over z, x), seq: 2 (over core), tensor: 2 (over y).
Axes of the slice: x: 2, y: 2, z: 4, core: 2. Of those that a mesh axis runs over, the one named last changes fastest.
Arguments:
- tokens: bfloat16 [4096, 768], P(('fsdp', 'seq', 'tensor')), may hold values from -6 to 6
- segments: int32 [4096], P('fsdp'), may hold values from 0 to 2, as said below
- grad_out: bfloat16 [4096, 768], P('fsdp'), may hold values from -6 to 6
- w_qkv: bfloat16 [3, 768, 768], P(None, 'fsdp', ('seq', 'tensor')), may hold values from -0.21875 to 0.21875
- b_qv: bfloat16 [2, 768], P(None, ('seq', 'tensor', 'fsdp')), may hold values from -3 to 3
- w_out: bfloat16 [768, 768], P(('seq', 'tensor'), 'fsdp'), may hold values from -0.875 to 0.875
- b_out: bfloat16 [768], P('fsdp'), may hold values from -2 to 2
- w_fc: bfloat16 [768, 3072], P('fsdp', ('seq', 'tensor')), may hold values from -0.21875 to 0.21875
- b_fc: bfloat16 [3072], P(('seq', 'tensor', 'fsdp')), may hold values from -3 to 3
- w_proj: bfloat16 [3072, 768], P(('seq', 'tensor'), 'fsdp'), may hold values from -0.109375 to 0.109375
- b_proj: bfloat16 [768], P('fsdp'), may hold values from -2 to 2
- ln1_gain: bfloat16 [768], P('fsdp'), may hold values from 0.5 to 1.5
- ln1_bias: bfloat16 [768], P('fsdp'), may hold values from -2 to 2
- ln2_gain: bfloat16 [768], P('fsdp'), may hold values from 0.5 to 1.5
- ln2_bias: bfloat16 [768], P('fsdp'), may hold values from -2 to 2
Outputs:
- output: bfloat16 [4096, 768], P(('fsdp', 'seq', 'tensor'))
- grad_tokens: float32 [4096, 768], P(('fsdp', 'seq', 'tensor'))
- grad_w_qkv: float32 [3, 768, 768], P(None, 'fsdp', ('seq', 'tensor'))
- grad_w_out: float32 [768, 768], P(('seq', 'tensor'), 'fsdp')
- grad_w_fc: float32 [768, 3072], P('fsdp', ('seq', 'tensor'))
- grad_w_proj: float32 [3072, 768], P(('seq', 'tensor'), 'fsdp')
- grad_b_qv: float32 [2, 768], P(None, ('seq', 'tensor', 'fsdp'))
- grad_b_out: float32 [768], P('fsdp')
- grad_b_fc: float32 [3072], P(('seq', 'tensor', 'fsdp'))
- grad_b_proj: float32 [768], P('fsdp')
- grad_ln1_gain: float32 [768], P('fsdp')
- grad_ln1_bias: float32 [768], P('fsdp')
- grad_ln2_gain: float32 [768], P('fsdp')
- grad_ln2_bias: float32 [768], P('fsdp')
The draws below stay inside these ranges and needn't reach their ends.
Inputs may be any that keep to these rules, and one draw needn't show every extreme that they name: `segments`: each sequence of 512 tokens holds three documents numbered 0, 1, 2 in order, each of 64 tokens or more; document 1 covers positions 224 to 287.
All inputs are finite; a program needn't handle non-finite values.
Results may differ from the reference program's by a relative error of at most 0.018.
Values may be sent and summed in bfloat16 or wider, within the bound.
No kernel may reach another device: no remote copies, remote signals or barrier semaphores. Data moves between devices by JAX's collectives and lax.ppermute only.
A program may use at most 64 MiB of HBM per device.

```python
import math
import jax
import jax.numpy as jnp
from jax import lax

D = 768
HEADS = 12
HEAD_DIM = 64
FF = 3072
SEQ_LEN = 512
TOKENS = 4096


def draw_segments(key, part):
    key = jax.random.fold_in(key, 11)
    key_low, key_high = jax.random.split(key)
    seq_count = TOKENS // SEQ_LEN
    low_cut = jax.random.randint(key_low, (seq_count,), SEQ_LEN // 8, SEQ_LEN // 2 - SEQ_LEN // 16 + 1)
    high_cut = jax.random.randint(key_high, (seq_count,), SEQ_LEN // 2 + SEQ_LEN // 16, SEQ_LEN - SEQ_LEN // 8 + 1)
    positions = jnp.arange(SEQ_LEN, dtype=jnp.int32)
    doc_ids = (positions[None, :] >= low_cut[:, None]).astype(jnp.int32) + (positions[None, :] >= high_cut[:, None]).astype(jnp.int32)
    return doc_ids.reshape(-1)


def with_spikes(entries, rng, source, target, parts, factor):
    owner, partner = [(jnp.arange(entries.shape[dim]) // (entries.shape[dim] // parts)).reshape([-1 if axis == dim else 1 for axis in range(entries.ndim)]) for dim in (source, target)]
    chosen = jax.random.permutation(rng, parts)[partner]
    strong = (owner == chosen) | (owner == (partner + parts // 2) % parts)
    return jnp.where(strong, factor * entries, entries)


def shard_levels(rng, dims, shards, smallest, largest):
    loudness = 1.0
    for dim, parts in shards:
        heights = jax.random.uniform(jax.random.fold_in(jax.random.fold_in(rng, 6), dim), (parts,), jnp.float32, smallest / len(shards), largest / len(shards))
        loudness = loudness * jnp.repeat(jnp.exp(heights), dims[dim] // parts).reshape((-1,) + (1,) * (len(dims) - 1 - dim))
    return loudness


def centred(own_key, dims, width, limit, shards=(), held_as=jnp.bfloat16):
    values = jax.random.normal(own_key, dims, jnp.float32) * width
    if len(shards) > 0:
        values = shard_levels(own_key, dims, shards, -0.22, 0.18) * values
    return jnp.clip(values, min=-limit, max=limit).astype(held_as)


def heavy_noise(stream_key, dims, width, limit, cuts, heavy, held_as=jnp.bfloat16):
    array = width * jax.random.normal(stream_key, dims, jnp.float32)
    if cuts:
        array = array * shard_levels(stream_key, dims, cuts, -0.22, 0.18)
    return jnp.clip(with_spikes(array, jax.random.fold_in(stream_key, 3), *heavy), -limit, limit).astype(held_as)


def setup_inputs(seed: int = 0) -> dict:
    keys = jax.random.split(jax.random.key(seed), 16)
    tokens = heavy_noise(keys[0], (TOKENS, D), 1.0, 6.0, ((0, 32),), (0, 1, 32, 2.75))
    segments = draw_segments(jax.random.fold_in(keys[15], 71), 0)
    grad_out = centred(keys[2], (TOKENS, D), 1.0, 6.0, ((0, 8),))
    w_qkv = centred(keys[3], (3, D, D), D ** -0.5, 0.21875, ((1, 8), (2, 4)))
    b_qv = centred(keys[4], (2, D), 0.5, 3.0, ((1, 32),))
    w_out = centred(keys[5], (D, D), (D // 16) ** -0.5, 0.875, ((0, 4), (1, 8)))
    b_out = centred(keys[6], (D,), 0.3, 2.0, ((0, 8),))
    w_fc = centred(keys[7], (D, FF), D ** -0.5, 0.21875, ((0, 8), (1, 4)))
    b_fc = centred(keys[8], (FF,), 0.5, 3.0, ((0, 32),))
    w_proj = centred(keys[9], (FF, D), FF ** -0.5, 0.109375, ((0, 4), (1, 8)))
    b_proj = centred(keys[10], (D,), 0.3, 2.0, ((0, 8),))
    ln1_gain = jnp.clip(1.0 + 0.1 * jax.random.normal(keys[11], (D,), jnp.float32), 0.5, 1.5).astype(jnp.bfloat16)
    ln1_bias = centred(keys[12], (D,), 0.3, 2.0, ((0, 8),))
    ln2_gain = jnp.clip(1.0 + 0.1 * jax.random.normal(keys[13], (D,), jnp.float32), 0.5, 1.5).astype(jnp.bfloat16)
    ln2_bias = centred(keys[14], (D,), 0.3, 2.0, ((0, 8),))
    return dict(tokens=tokens, segments=segments, grad_out=grad_out, w_qkv=w_qkv, b_qv=b_qv, w_out=w_out, b_out=b_out, w_fc=w_fc, b_fc=b_fc, w_proj=w_proj, b_proj=b_proj, ln1_gain=ln1_gain, ln1_bias=ln1_bias, ln2_gain=ln2_gain, ln2_bias=ln2_bias)


@jax.custom_vjp
def low(v):
    return lax.optimization_barrier(v.astype(jnp.bfloat16)).astype(jnp.float32)

@jax.custom_vjp
def low_back(v):
    return v

def low_keep(v):
    return (low(v), None)

def low_pass(kept, grad):
    return (grad,)

def back_keep(v):
    return (v, None)

def back_low(kept, grad):
    return (low(grad),)
low.defvjp(low_keep, low_pass)
low_back.defvjp(back_keep, back_low)

def norm_rows(values, gain, shift):
    center = values - lax.optimization_barrier(jnp.mean(values, axis=-1, keepdims=True))
    spread = lax.optimization_barrier(jnp.mean(center * center, axis=-1, keepdims=True))
    return center * lax.rsqrt(spread + 1e-05) * gain + shift

def matmul_high(left, right):
    return jnp.dot(left, right, precision=lax.Precision.HIGHEST)

def attend(queries, keys_all, values_all, doc_ids):
    block_rows = min(512, SEQ_LEN)
    key_pos = jnp.arange(SEQ_LEN, dtype=jnp.int32)

    def query_block(number):
        offset = number * block_rows
        q_block = lax.dynamic_slice_in_dim(queries, offset, block_rows, 0)
        doc_block = lax.dynamic_slice_in_dim(doc_ids, offset, block_rows, 0)
        query_pos = offset + jnp.arange(block_rows, dtype=jnp.int32)
        allowed = (doc_block[:, None] == doc_ids[None, :]) & (key_pos[None, :] <= query_pos[:, None])
        scores = low_back(jnp.einsum('qhd,khd->hqk', q_block, keys_all, precision=lax.Precision.HIGHEST) * 0.125)
        scores = jnp.where(allowed[None], scores, -1e+30)
        row_top = lax.optimization_barrier(jnp.max(scores, axis=-1, keepdims=True))
        log_norm = row_top + jnp.log(lax.optimization_barrier(jnp.sum(jnp.exp(scores - row_top), axis=-1, keepdims=True)))
        probs = low(jnp.exp(scores - log_norm))
        return jnp.einsum('hqk,khd->qhd', probs, values_all, precision=lax.Precision.HIGHEST)
    mixed = lax.map(jax.checkpoint(query_block), jnp.arange(SEQ_LEN // block_rows, dtype=jnp.int32))
    return mixed.reshape(SEQ_LEN, HEADS * HEAD_DIM)

def residual_block(inputs, doc_ids, w_qkv, b_qv, w_out, b_out, w_fc, b_fc, w_proj, b_proj, gain_one, shift_one, gain_two, shift_two):
    normed = low(norm_rows(inputs, gain_one, shift_one))
    queries = low(low_back(matmul_high(normed, w_qkv[0]) + b_qv[0]))
    keys_all = low(low_back(matmul_high(normed, w_qkv[1])))
    values_all = low(low_back(matmul_high(normed, w_qkv[2]) + b_qv[1]))
    seq_shape = (doc_ids.shape[0], SEQ_LEN, HEADS, HEAD_DIM)
    mixed = lax.map(lambda items: attend(items[0], items[1], items[2], items[3]), (queries.reshape(seq_shape), keys_all.reshape(seq_shape), values_all.reshape(seq_shape), doc_ids))
    attn_rows = low(low_back(mixed.reshape(-1, D)))
    middle = inputs + low_back(matmul_high(attn_rows, w_out)) + b_out
    normed_two = low(norm_rows(middle, gain_two, shift_two))
    hidden = low_back(matmul_high(normed_two, w_fc) + b_fc)
    active = low(jax.nn.gelu(hidden, approximate=True))
    return middle + low_back(matmul_high(active, w_proj)) + b_proj

def reference(tokens, segments, grad_out, w_qkv, b_qv, w_out, b_out, w_fc, b_fc, w_proj, b_proj, ln1_gain, ln1_bias, ln2_gain, ln2_bias):
    all_seqs = TOKENS // SEQ_LEN
    group_seqs = math.gcd(max(1, 4096 // SEQ_LEN), all_seqs)
    group_count = all_seqs // group_seqs
    group_rows = group_seqs * SEQ_LEN
    inputs_all = tokens.astype(jnp.float32).reshape(group_count, group_rows, D)
    cotangents = grad_out.astype(jnp.float32).reshape(group_count, group_rows, D)
    doc_groups = segments.reshape(group_count, group_seqs, SEQ_LEN)
    weights = tuple((item.astype(jnp.float32) for item in (w_qkv, b_qv, w_out, b_out, w_fc, b_fc, w_proj, b_proj, ln1_gain, ln1_bias, ln2_gain, ln2_bias)))

    def group_step(totals, inputs):
        input_block, cot_block, doc_block = inputs

        def forward(rows_in, *params):
            return residual_block(rows_in, doc_block, *params)
        result, pullback = jax.vjp(forward, input_block, *weights)
        gradients = pullback(cot_block)
        totals = tuple((acc + new for acc, new in zip(totals, gradients[1:])))
        return (totals, (result, gradients[0]))
    zero_grads = tuple((jnp.zeros(item.shape, jnp.float32) for item in weights))
    totals, (outputs_all, input_grads) = lax.scan(group_step, zero_grads, (inputs_all, cotangents, doc_groups))
    return (outputs_all.reshape(TOKENS, D).astype(jnp.bfloat16), input_grads.reshape(TOKENS, D), totals[0], totals[2], totals[4], totals[6], totals[1], totals[3], totals[5], totals[7], totals[8], totals[9], totals[10], totals[11])
```

```python
import jax
import jax.numpy as jnp
from jax import lax
from jax.sharding import PartitionSpec as P

HEAD_DIM = 64
DIRECT_LIMIT = 8
LOW = jnp.bfloat16
F32 = jnp.float32


def norm_parts(values):
    center = values - jnp.mean(values, axis=-1, keepdims=True)
    spread = jnp.mean(center * center, axis=-1, keepdims=True)
    inverse = lax.rsqrt(spread + 1e-05)
    return center * inverse, inverse


def norm_back(cot, scaled, inverse, gain):
    inner = cot * gain
    first = jnp.mean(inner, axis=-1, keepdims=True)
    second = jnp.mean(inner * scaled, axis=-1, keepdims=True)
    return (inner - first - scaled * second) * inverse


def gelu_tanh(values):
    return jax.nn.gelu(values, approximate=True)


def dot(left, right, left_dim, right_dim):
    return lax.dot_general(
        left, right, (((left_dim,), (right_dim,)), ((), ())), preferred_element_type=F32
    )


def shifted(value, step):
    size = lax.axis_size("fsdp")
    return lax.ppermute(value, "fsdp", [(i, (i + step) % size) for i in range(size)])


def swap(value, axis):
    return lax.ppermute(value, axis, [(0, 1), (1, 0)])


def gather_chunks(chunk):
    size = lax.axis_size("fsdp")
    if size > DIRECT_LIMIT:
        return lax.all_gather(chunk, "fsdp", axis=0, tiled=False)
    return jnp.stack([chunk] + [shifted(chunk, -step) for step in range(1, size)])


def scatter_chunks(chunks):
    size = lax.axis_size("fsdp")
    if size > DIRECT_LIMIT:
        return lax.psum_scatter(chunks, "fsdp", scatter_dimension=0, tiled=False)
    total = chunks[0]
    low = chunks.astype(LOW)
    for step in range(1, size):
        total = total + shifted(low[step], step).astype(F32)
    return total


def turn(value, count, axis):
    return jnp.roll(value, -count, axis=axis)


def local(
    tokens,
    segments,
    grad_out,
    w_qkv,
    b_qv,
    w_out,
    b_out,
    w_fc,
    b_fc,
    w_proj,
    b_proj,
    ln1_gain,
    ln1_bias,
    ln2_gain,
    ln2_bias,
):
    size = lax.axis_size("fsdp")
    me = lax.axis_index("fsdp")
    chunk_rows = w_fc.shape[0]
    width = tokens.shape[1]
    own_rows = tokens.shape[0]
    seq_rows = segments.shape[0]
    hidden_cols = w_fc.shape[1]
    head_cols = w_out.shape[0]
    heads = head_cols // HEAD_DIM
    qkv_cols = 3 * head_cols
    offset = me * chunk_rows if size <= DIRECT_LIMIT else 0 * me
    place = lax.axis_index("seq") * 2 + lax.axis_index("tensor")

    vectors = jnp.concatenate(
        [b_out, b_proj, ln1_gain, ln1_bias, ln2_gain, ln2_bias, b_qv.reshape(-1), b_fc]
    )
    vector_rows = -(-vectors.shape[0] // qkv_cols)
    vectors = jnp.pad(vectors, (0, vector_rows * qkv_cols - vectors.shape[0]))
    first = jnp.concatenate(
        [w_qkv[0], w_qkv[1], w_qkv[2]], axis=1
    )
    first = jnp.concatenate([first, vectors.reshape(vector_rows, qkv_cols)], axis=0)
    second = jnp.concatenate([w_out.T, w_fc, w_proj.T], axis=1)
    own_tokens = turn(tokens, offset, 1)

    near = swap(own_tokens, "tensor")
    pair = jnp.concatenate([own_tokens, near])
    seq_tokens = jnp.concatenate([pair, swap(pair, "seq")])

    first_all = gather_chunks(first)
    second_all = gather_chunks(second)
    qkv_all = first_all[:, :chunk_rows].reshape(width, qkv_cols)
    vec_all = first_all[:, chunk_rows:].reshape(size, -1).astype(F32)
    d_vec = vec_all[:, : 6 * chunk_rows].reshape(size, 6, chunk_rows).transpose(1, 0, 2).reshape(6, width)
    bout_all, bproj_all, gain_one, shift_one, gain_two, shift_two = [d_vec[i] for i in range(6)]
    qv_count = b_qv.shape[1]
    rest = jnp.roll(vec_all[:, 6 * chunk_rows :], offset // chunk_rows, axis=0)
    qv_all = rest[:, : 2 * qv_count].reshape(size, 2, qv_count).transpose(1, 0, 2).reshape(2, head_cols)
    bfc_all = rest[:, 2 * qv_count : 2 * qv_count + chunk_rows * 0 + b_fc.shape[0]].reshape(hidden_cols)

    second_flat = second_all.reshape(width, -1)
    wo_own = second_flat[:, :head_cols]
    wf = second_flat[:, head_cols : head_cols + hidden_cols]
    wp = second_flat[:, head_cols + hidden_cols :]
    wo_pair = jnp.concatenate([wo_own, swap(wo_own, "tensor")], axis=1)
    wo_full = jnp.concatenate([wo_pair, swap(wo_pair, "seq")], axis=1)

    blocks = [place ^ b for b in range(4)]

    def in_order(value):
        return jnp.concatenate(
            [lax.dynamic_slice_in_dim(value, b * own_rows, own_rows, 0) for b in blocks]
        )

    docs = in_order(segments)
    cot = turn(in_order(grad_out), offset, 1)
    positions = jnp.concatenate([b * own_rows + jnp.arange(own_rows, dtype=jnp.int32) for b in blocks])
    allowed = (docs[:, None] == docs[None, :]) & (positions[None, :] <= positions[:, None])

    inputs = seq_tokens.astype(F32)
    scaled_one, inverse_one = norm_parts(inputs)
    normed = (scaled_one * gain_one + shift_one).astype(LOW)
    bias_row = jnp.concatenate([qv_all[0], jnp.zeros((head_cols,), F32), qv_all[1]])
    qkv_low = (dot(normed, qkv_all, 1, 0) + bias_row).astype(LOW)
    queries, keys, values = [
        qkv_low[:, i * head_cols : (i + 1) * head_cols].reshape(seq_rows, heads, HEAD_DIM)
        for i in range(3)
    ]
    scores = jnp.einsum("qhd,khd->hqk", queries, keys, preferred_element_type=F32) * 0.125
    scores = jnp.where(allowed[None], scores, -1e30)
    top = jnp.max(scores, axis=-1, keepdims=True)
    log_norm = top + jnp.log(jnp.sum(jnp.exp(scores - top), axis=-1, keepdims=True))
    probs = jnp.exp(scores - log_norm)
    probs_low = probs.astype(LOW)
    mixed = (
        jnp.einsum("hqk,khd->qhd", probs_low, values, preferred_element_type=F32)
        .astype(LOW)
        .reshape(seq_rows, head_cols)
    )

    def cross(value):
        part = value.reshape(4, own_rows, -1)
        return jnp.concatenate([part[1], part[0], part[3], part[2]])

    mixed_pair = jnp.concatenate([mixed, cross(swap(mixed, "tensor"))], axis=1)
    other_pair = swap(mixed_pair, "seq")
    half = 2 * own_rows
    other_pair = jnp.concatenate([other_pair[half:], other_pair[:half]])
    mixed_full = jnp.concatenate([mixed_pair, other_pair], axis=1)
    middle = inputs + dot(mixed_full, wo_full, 1, 1) + bout_all
    scaled_two, inverse_two = norm_parts(middle)
    normed_two = (scaled_two * gain_two + shift_two).astype(LOW)
    hidden = dot(normed_two, wf, 1, 0) + bfc_all
    active, gelu_pull = jax.vjp(gelu_tanh, hidden)
    active_low = active.astype(LOW)
    grad_hidden = gelu_pull(dot(cot, wp, 1, 0))[0].astype(LOW)

    def sum_half(partial):
        return partial[:half] + swap(partial[half:].astype(LOW), "seq").astype(F32)

    part_two = sum_half(dot(grad_hidden, wf, 1, 1))
    far = swap(part_two.astype(LOW), "tensor").astype(F32)
    grad_normed_two = part_two + jnp.concatenate([far[own_rows:], far[:own_rows]])
    cot_half = cot[:half].astype(F32)
    grad_middle = cot_half + norm_back(
        grad_normed_two, scaled_two[:half], inverse_two[:half], gain_two
    )
    grad_mid_half = grad_middle.astype(LOW)
    seq_grad_mid = jnp.concatenate([grad_mid_half, swap(grad_mid_half, "seq")])

    out_half = sum_half(dot(active_low, wp, 1, 1))
    out_own = out_half[:own_rows] + swap(out_half[own_rows:].astype(LOW), "tensor").astype(F32)
    result = turn((middle[:own_rows] + out_own + bproj_all).astype(LOW), width - offset, 1)

    grad_ff = jnp.concatenate([dot(normed_two, grad_hidden, 0, 0), dot(cot, active_low, 0, 0)], axis=1)
    sum_ff = scatter_chunks(grad_ff.reshape(size, chunk_rows, -1))

    grad_wo = dot(seq_grad_mid, mixed, 0, 0)
    grad_attn = dot(seq_grad_mid, wo_own, 1, 0).astype(LOW).reshape(seq_rows, heads, HEAD_DIM)
    grad_probs = jnp.einsum("qhd,khd->hqk", grad_attn, values, preferred_element_type=F32)
    inner = jnp.sum(probs * grad_probs, axis=-1, keepdims=True)
    grad_scores = (probs * (grad_probs - inner)).astype(LOW)
    query_grad = jnp.einsum("hqk,khd->qhd", grad_scores, keys, preferred_element_type=F32) * 0.125
    key_grad = jnp.einsum("hqk,qhd->khd", grad_scores, queries, preferred_element_type=F32) * 0.125
    value_grad = jnp.einsum("hqk,qhd->khd", probs_low, grad_attn, preferred_element_type=F32)
    grad_qkv = jnp.concatenate(
        [item.reshape(seq_rows, head_cols).astype(LOW) for item in (query_grad, key_grad, value_grad)],
        axis=1,
    )
    grad_wqkv = dot(normed, grad_qkv, 0, 0)
    part_normed = dot(grad_qkv, qkv_all, 1, 1)
    half_normed = sum_half(part_normed)
    grad_normed = half_normed[:own_rows] + swap(half_normed[own_rows:].astype(LOW), "tensor").astype(F32)
    own_scaled = scaled_one[:own_rows]
    grad_inputs = grad_middle[:own_rows] + norm_back(
        grad_normed, own_scaled, inverse_one[:own_rows], gain_one
    )
    grad_inputs = turn(grad_inputs, width - offset, 1)

    own_two = grad_normed_two[:own_rows]
    sums = jnp.stack(
        [
            jnp.sum(grad_middle[:own_rows], axis=0),
            jnp.sum(cot_half[:own_rows], axis=0),
            jnp.sum(part_normed * scaled_one, axis=0),
            jnp.sum(part_normed, axis=0),
            jnp.sum(own_two * scaled_two[:own_rows], axis=0),
            jnp.sum(own_two, axis=0),
        ]
    )
    sums = sums + swap(sums, "tensor")
    sums = sums + swap(sums, "seq")
    d_sums = sums.reshape(6, size, chunk_rows).transpose(1, 0, 2).reshape(size, -1)
    grad_qv = jnp.sum(grad_qkv.astype(F32), axis=0)
    qv_sums = (
        jnp.stack([grad_qv[:head_cols], grad_qv[2 * head_cols :]])
        .reshape(2, size, qv_count)
        .transpose(1, 0, 2)
        .reshape(size, -1)
    )
    fc_sums = jnp.sum(grad_hidden.astype(F32), axis=0).reshape(size, -1)
    rest_sums = jnp.roll(jnp.concatenate([qv_sums, fc_sums], axis=1), -(offset // chunk_rows), axis=0)
    vec_sums = jnp.concatenate([d_sums, rest_sums], axis=1)
    last_cols = qkv_cols + head_cols
    vec_count = vec_sums.shape[1]
    vec_rows = -(-vec_count // last_cols)
    vec_sums = jnp.pad(vec_sums, ((0, 0), (0, vec_rows * last_cols - vec_count)))
    last = jnp.concatenate([grad_wqkv, grad_wo], axis=1).reshape(size, chunk_rows, last_cols)
    last = jnp.concatenate([last, vec_sums.reshape(size, vec_rows, last_cols)], axis=1)
    sum_last = scatter_chunks(last)

    own_vec = sum_last[chunk_rows:].reshape(-1)
    d_own = own_vec[: 6 * chunk_rows].reshape(6, chunk_rows)
    qv_own = own_vec[6 * chunk_rows : 6 * chunk_rows + 2 * qv_count].reshape(2, qv_count)
    fc_own = own_vec[6 * chunk_rows + 2 * qv_count : vec_count]
    wqkv_own = jnp.stack(
        [sum_last[:chunk_rows, i * head_cols : (i + 1) * head_cols] for i in range(3)]
    )
    return (
        result,
        grad_inputs,
        wqkv_own,
        sum_last[:chunk_rows, qkv_cols:].T,
        sum_ff[:, :hidden_cols],
        sum_ff[:, hidden_cols:].T,
        qv_own,
        d_own[0],
        fc_own,
        d_own[1],
        d_own[2],
        d_own[3],
        d_own[4],
        d_own[5],
    )


def solution(mesh):
    in_specs = (
        P(("fsdp", "seq", "tensor"), None),
        P("fsdp"),
        P("fsdp", None),
        P(None, "fsdp", ("seq", "tensor")),
        P(None, ("seq", "tensor", "fsdp")),
        P(("seq", "tensor"), "fsdp"),
        P("fsdp"),
        P("fsdp", ("seq", "tensor")),
        P(("seq", "tensor", "fsdp")),
        P(("seq", "tensor"), "fsdp"),
        P("fsdp"),
        P("fsdp"),
        P("fsdp"),
        P("fsdp"),
        P("fsdp"),
    )
    out_specs = (
        P(("fsdp", "seq", "tensor"), None),
        P(("fsdp", "seq", "tensor"), None),
        P(None, "fsdp", ("seq", "tensor")),
        P(("seq", "tensor"), "fsdp"),
        P("fsdp", ("seq", "tensor")),
        P(("seq", "tensor"), "fsdp"),
        P(None, ("seq", "tensor", "fsdp")),
        P("fsdp"),
        P(("seq", "tensor", "fsdp")),
        P("fsdp"),
        P("fsdp"),
        P("fsdp"),
        P("fsdp"),
        P("fsdp"),
    )
    return jax.shard_map(local, mesh=mesh, in_specs=in_specs, out_specs=out_specs, check_vma=False)
```

```python
import functools

import jax
import jax.numpy as jnp
import numpy as np
from jax import lax
from jax.experimental import pallas as pl
from jax.experimental.pallas import tpu as pltpu
from jax.sharding import PartitionSpec as P

HEAD_DIM = 64
DIRECT_SIZE = 8
STEPS = ((0, 0), (1, 0), (3, 1), (3, 0), (1, 1), (0, 1), (2, 0), (2, 1))
VEC_COLS = 128
LOW = jnp.bfloat16
F32 = jnp.float32
GELU_SCALE = float(np.sqrt(2.0 / np.pi))


def shape(rows, cols, dtype):
    return jax.ShapeDtypeStruct((rows, cols), dtype)


def on_core(body, outs, scalars, arrays, scratch=(), flops=0, limit=48):
    specs = [pl.BlockSpec(memory_space=pltpu.SMEM)] * len(scalars)
    specs += [pl.BlockSpec(memory_space=pltpu.VMEM)] * len(arrays)
    moved = sum(int(np.prod(a.shape)) * a.dtype.itemsize for a in arrays) + sum(
        int(np.prod(o.shape)) * o.dtype.itemsize for o in outs
    )
    return pl.pallas_call(
        body,
        out_shape=tuple(outs),
        in_specs=specs,
        out_specs=tuple(pl.BlockSpec(memory_space=pltpu.VMEM) for _ in outs),
        scratch_shapes=list(scratch),
        compiler_params=pltpu.CompilerParams(vmem_limit_bytes=limit * 2**20),
        cost_estimate=pl.CostEstimate(flops=flops, bytes_accessed=moved, transcendentals=0),
    )(*scalars, *arrays)


def dot(left, right, left_dim, right_dim):
    return lax.dot_general(
        left, right, (((left_dim,), (right_dim,)), ((), ())), preferred_element_type=F32
    )


def norm_parts(values):
    center = values - jnp.mean(values, axis=-1, keepdims=True)
    spread = jnp.mean(center * center, axis=-1, keepdims=True)
    inverse = lax.rsqrt(spread + 1e-05)
    return center * inverse, inverse


def norm_back(cot, scaled, inverse, gain):
    inner = cot * gain
    first = jnp.mean(inner, axis=-1, keepdims=True)
    second = jnp.mean(inner * scaled, axis=-1, keepdims=True)
    return (inner - first - scaled * second) * inverse


def turned(value):
    count = value.shape[1]
    row = lax.broadcasted_iota(jnp.int32, (count, count), 0)
    col = lax.broadcasted_iota(jnp.int32, (count, count), 1)
    return dot((row == col).astype(F32).astype(LOW), value, 1, 1).astype(LOW)


def turned_wide(value):
    rows = value.shape[0]
    lack = -rows % 128
    if lack:
        value = jnp.concatenate([value, jnp.zeros((lack, value.shape[1]), value.dtype)], axis=0)
    return value.T[:, :rows]


def swap(value, axis):
    return lax.ppermute(value, axis, [(0, 1), (1, 0)])


def send(value, turn, flip):
    pairs = [(i, (i // 2 + turn) % 4 * 2 + (i % 2 ^ flip)) for i in range(DIRECT_SIZE)]
    return lax.ppermute(value, "fsdp", pairs)


def after(value, *earlier):
    return lax.optimization_barrier((value, *earlier))[0]


def pieces_of(chunk):
    ahead = send(chunk, 3, 0)
    behind = send(chunk, 1, 1)
    rest = [send(chunk, 1, 0), send(chunk, 3, 1), send(chunk, 0, 1)]
    return [chunk, ahead, behind, *rest, send(ahead, 3, 0), send(behind, 1, 0)]


def sums_of(pieces):
    own, ahead, behind, near_behind, near_ahead, other, far, far_other = pieces
    passed = send(far, 1, 0), send(far_other, 3, 0)
    rest = [send(near_behind, 3, 0), send(near_ahead, 1, 1), send(other, 0, 1)]
    ahead, behind = [
        (mine.astype(F32) + got.astype(F32)).astype(LOW) for mine, got in zip((ahead, behind), passed)
    ]
    return [own, *rest, send(ahead, 1, 0), send(behind, 3, 1)]


def row_start(me, step, rows):
    turn, flip = STEPS[step]
    pair = lax.rem(lax.div(me, 2) + turn, 4)
    return pl.multiple_of((pair * 2 + (lax.rem(me, 2) ^ flip)) * rows, rows)


def pack_first_body(wqkv, wout, vecs, out):
    rows = wqkv.shape[1]
    cols = turned_wide(vecs[...].astype(F32))[:rows].astype(LOW)
    lack = jnp.zeros((rows, VEC_COLS - cols.shape[1]), LOW)
    out[...] = jnp.concatenate(
        [cols, lack, wqkv[0], wqkv[1], wqkv[2], turned(wout[...])], axis=1
    )


def pack_second_body(wfc, wproj, out):
    out[...] = jnp.concatenate([wfc[...], turned(wproj[...])], axis=1)


def open_first_body(size, scal, *refs):
    pieces, (sel, wqkv, wo, rows, bias, cols) = refs[:size], refs[size:]
    chunk = pieces[0].shape[0]
    split = VEC_COLS + wqkv.shape[1]
    for step, piece in enumerate(pieces):
        place = pl.ds(row_start(scal[0], step, chunk) if size > 1 else 0, chunk)
        value = piece[...]
        cols[place, :] = value[:, :VEC_COLS].astype(F32)
        wqkv[place, :] = value[:, VEC_COLS:split]
        wo[place, :] = value[:, split:]
    wide = cols[...].T
    rows[...] = wide[:8]
    bias[...] = dot(wide[:8].astype(LOW), sel[...], 1, 0)


def open_second_body(size, scal, *refs):
    pieces, (grad, wf, wp, da, cot) = refs[:size], refs[size:]
    chunk = pieces[0].shape[0]
    cols = wf.shape[1]
    own = cot.shape[0] // 4
    for step, piece in enumerate(pieces):
        place = pl.ds(row_start(scal[0], step, chunk) if size > 1 else 0, chunk)
        wf[place, :] = piece[:, :cols]
        wp[place, :] = piece[:, cols:]
    for block in range(4):
        start = pl.multiple_of((scal[1] ^ block) * own, own)
        cot[block * own : (block + 1) * own, :] = grad[pl.ds(start, own), :]
    da[...] = dot(cot[...], wp[...], 1, 0)


def fill_mask(mask, doc_col, doc_row, pos_col, pos_row):
    total = mask.shape[0]
    for low in range(0, total, 128):
        part = slice(low, low + 128)
        seen = (doc_col[part, :] == doc_row[...]) & (pos_row[...] <= pos_col[part, :])
        mask[part, :] = jnp.where(seen, 0.0, -1e30)


def attend_body(
    own, near, pair, wqkv, bias, rows, doc_col, doc_row, pos_col, pos_row,
    qkv, mixed, lse, normed, mask,
):
    total = qkv.shape[0]
    part = own.shape[0]
    gain, shift = rows[2:3, :], rows[3:4, :]
    sources = (own[...], near[...], pair[:part, :], pair[part:, :])
    for number, source in enumerate(sources):
        scaled, _ = norm_parts(source.astype(F32))
        normed[number * part : (number + 1) * part, :] = (scaled * gain + shift).astype(LOW)
    qkv[...] = (dot(normed[...], wqkv[...], 1, 0) + bias[7:8, :]).astype(LOW)
    fill_mask(mask, doc_col, doc_row, pos_col, pos_row)
    width = qkv.shape[1] // 3
    heads = width // HEAD_DIM
    step = total // 2
    for low in range(0, total, step):
        here = slice(low, low + step)
        found, norms = [], []
        for head in range(heads):
            at = head * HEAD_DIM
            query = qkv[here, at : at + HEAD_DIM]
            key = qkv[:, width + at : width + at + HEAD_DIM]
            value = qkv[:, 2 * width + at : 2 * width + at + HEAD_DIM]
            scores = dot(query, key, 1, 1) * 0.125 + mask[here, :]
            top = jnp.max(scores, axis=-1, keepdims=True)
            raised = jnp.exp(scores - top)
            total_raised = jnp.sum(raised, axis=-1, keepdims=True)
            probs = (raised * (1.0 / total_raised)).astype(LOW)
            found.append(dot(probs, value, 1, 0))
            norms.append(top + jnp.log(total_raised))
        mixed[here, :] = jnp.concatenate(found, axis=1).astype(LOW)
        for head in range(heads):
            lse[here, head : head + 1] = norms[head]


def feed_body(
    own, near, pair, mixed_own, mixed_near, mixed_pair, wo_own, wo_near, wo_pair, wf, rows, da,
    keep, send, middle, normed, active, grad_hidden,
):
    part = own.shape[0]
    half = 2 * part
    head_cols = mixed_own.shape[1]
    for number in range(2):
        here = slice(number * half, (number + 1) * half)
        if number == 0:
            source = jnp.concatenate([own[...], near[...]], axis=0)
            swapped = slice(half, 2 * half)
        else:
            source = pair[...]
            swapped = slice(0, half)
        low = number * half
        across = jnp.concatenate(
            [mixed_near[low + part : low + half, :], mixed_near[low : low + part, :]], axis=0
        )
        total = source.astype(F32) + rows[0:1, :]
        total += dot(mixed_own[here, :], wo_own[...], 1, 1)
        total += dot(across, wo_near[...], 1, 1)
        total += dot(mixed_pair[swapped, :], wo_pair[...], 1, 1)
        if number == 0:
            middle[...] = total
        scaled, _ = norm_parts(total)
        low_norm = (scaled * rows[4:5, :] + rows[5:6, :]).astype(LOW)
        normed[here, :] = low_norm
        hidden = dot(low_norm, wf[...], 1, 0) + rows[6:7, :]
        square = hidden * hidden
        bent = jnp.tanh(GELU_SCALE * hidden * (1.0 + 0.044715 * square))
        rise = 0.5 * (1.0 + bent)
        active[here, :] = (hidden * rise).astype(LOW)
        slope = rise + 0.5 * hidden * (1.0 - bent * bent) * (
            GELU_SCALE * (1.0 + 3 * 0.044715 * square)
        )
        grad_low = (da[here, :] * slope).astype(LOW)
        grad_hidden[here, :] = grad_low
        back = dot(grad_low, wf[...], 1, 1)
        if number == 0:
            keep[...] = back
        else:
            send[...] = back.astype(LOW)


def put_pieces(me, whole, outs):
    size = len(outs)
    if size == 1:
        outs[0][...] = whole[...]
        return
    chunk = outs[0].shape[0]
    for step, out in enumerate(outs):
        value = whole[pl.ds(row_start(me, step, chunk), chunk), :]
        out[...] = value.astype(out.dtype)


def feed_grad_body(size, scal, active, wp, normed, grad_hidden, cot, *refs):
    keep, send, fc_sum = refs[:3]
    pieces, whole = refs[3 : 3 + size], refs[3 + size]
    half = keep.shape[0]
    cols = wp.shape[1]
    whole[:, :cols] = dot(normed[...], grad_hidden[...], 0, 0)
    whole[:, cols:] = dot(cot[...], active[...], 0, 0)
    put_pieces(scal[0], whole, pieces)
    keep[...] = dot(active[:half, :], wp[...], 1, 1)
    send[...] = dot(active[half:, :], wp[...], 1, 1).astype(LOW)
    fc_sum[...] = jnp.sum(grad_hidden[...].astype(F32), axis=0, keepdims=True)


def middle_body(part_two, far, middle, cot, rows, grad_low, grad_own, early):
    own = grad_own.shape[0]
    flipped = jnp.concatenate([far[own:, :], far[:own, :]], axis=0).astype(F32)
    grad = part_two[...] + flipped
    scaled, inverse = norm_parts(middle[...])
    cotangent = cot[: 2 * own, :].astype(F32)
    total = cotangent + norm_back(grad, scaled, inverse, rows[4:5, :])
    grad_low[...] = total.astype(LOW)
    grad_own[...] = total[:own]
    add = functools.partial(jnp.sum, axis=0, keepdims=True)
    empty = jnp.zeros((2, total.shape[1]), F32)
    early[...] = jnp.concatenate(
        [add(total[:own]), add(cotangent[:own]), empty, add(grad[:own] * scaled[:own]), add(grad[:own]), empty],
        axis=0,
    )


def attend_back_body(
    grad_half, grad_other, wo, wqkv, qkv, lse, own, near, pair, early, doc_col, doc_row, pos_col, pos_row,
    keep, send, grad_qkv, late, qkv_sum, mask,
):
    total = qkv.shape[0]
    half = total // 2
    part = own.shape[0]
    width = qkv.shape[1] // 3
    heads = width // HEAD_DIM
    fill_mask(mask, doc_col, doc_row, pos_col, pos_row)
    grad_attn = [dot(g[...], wo[...], 1, 0).astype(LOW) for g in (grad_half, grad_other)]
    query_grads = [[], []]
    key_grads, value_grads = [], []
    for head in range(heads):
        at = head * HEAD_DIM
        key = qkv[:, width + at : width + at + HEAD_DIM]
        value = qkv[:, 2 * width + at : 2 * width + at + HEAD_DIM]
        key_grad = value_grad = None
        for number in range(2):
            here = slice(number * half, (number + 1) * half)
            query = qkv[here, at : at + HEAD_DIM]
            grad = grad_attn[number][:, at : at + HEAD_DIM]
            scores = dot(query, key, 1, 1) * 0.125 + mask[here, :]
            probs = jnp.exp(scores - lse[here, head : head + 1])
            grad_probs = dot(grad, value, 1, 1)
            inner = jnp.sum(probs * grad_probs, axis=-1, keepdims=True)
            grad_scores = (probs * (grad_probs - inner)).astype(LOW)
            query_grads[number].append(dot(grad_scores, key, 1, 0) * 0.125)
            more_key = dot(grad_scores, query, 0, 0)
            more_value = dot(probs.astype(LOW), grad, 0, 0)
            key_grad = more_key if key_grad is None else key_grad + more_key
            value_grad = more_value if value_grad is None else value_grad + more_value
        key_grads.append(key_grad * 0.125)
        value_grads.append(value_grad)
    for number in range(2):
        here = slice(number * half, (number + 1) * half)
        grad_qkv[here, :] = jnp.concatenate(
            query_grads[number] + [k[here] for k in key_grads] + [v[here] for v in value_grads], axis=1
        ).astype(LOW)
    gain_sum = shift_sum = 0.0
    for number in range(2):
        here = slice(number * half, (number + 1) * half)
        back = dot(grad_qkv[here, :], wqkv[...], 1, 1)
        source = jnp.concatenate([own[...], near[...]], axis=0) if number == 0 else pair[...]
        scaled, _ = norm_parts(source.astype(F32))
        gain_sum += jnp.sum(back * scaled, axis=0, keepdims=True)
        shift_sum += jnp.sum(back, axis=0, keepdims=True)
        if number == 0:
            keep[...] = back
        else:
            send[...] = back.astype(LOW)
    late[...] = jnp.concatenate([early[:2, :], gain_sum, shift_sum, early[4:, :]], axis=0)
    sums = jnp.sum(grad_qkv[...].astype(F32), axis=0, keepdims=True)
    qkv_sum[...] = jnp.concatenate([sums, jnp.zeros((7, sums.shape[1]), F32)], axis=0)


def last_grad_body(
    size, scal, grad_half, grad_other, mixed, own, near, pair, rows, grad_qkv, late, fc_sum, qkv_sum, sel, *refs
):
    pieces, (whole, normed) = refs[:size], refs[size:]
    part = own.shape[0]
    half = 2 * part
    sources = (own[...], near[...], pair[:part, :], pair[part:, :])
    for number, source in enumerate(sources):
        scaled, _ = norm_parts(source.astype(F32))
        normed[number * part : (number + 1) * part, :] = (scaled * rows[2:3, :] + rows[3:4, :]).astype(LOW)
    qkv_cols = grad_qkv.shape[1]
    split = VEC_COLS + qkv_cols
    placed = lax.dot_general(
        qkv_sum[...], sel[...].astype(F32), (((1,), (1,)), ((), ())),
        preferred_element_type=F32, precision=lax.Precision.HIGHEST,
    )
    line = jnp.concatenate([late[:6, :], fc_sum[...], placed[:1]], axis=0)
    lack = jnp.zeros((VEC_COLS - 8, line.shape[1]), F32)
    whole[:, :VEC_COLS] = jnp.concatenate([line, lack], axis=0).T
    whole[:, VEC_COLS:] = jnp.concatenate(
        [
            dot(normed[...], grad_qkv[...], 0, 0),
            dot(grad_half[...], mixed[:half, :], 0, 0) + dot(grad_other[...], mixed[half:, :], 0, 0),
        ],
        axis=1,
    )
    put_pieces(scal[0], whole, pieces)


def input_body(keep, far, middle_grad, own, rows, out):
    part = own.shape[0]
    grad = keep[:part, :] + far[...].astype(F32)
    scaled, inverse = norm_parts(own[...].astype(F32))
    out[...] = middle_grad[...] + norm_back(grad, scaled, inverse, rows[2:3, :])


def total_of(refs):
    total = refs[0][...]
    for ref in refs[1:]:
        total = total + ref[...].astype(F32)
    return total


def sum_feed_body(size, *refs):
    total = total_of(refs[:size])
    wfc, wproj = refs[size:]
    cols = wfc.shape[1]
    wfc[...] = total[:, :cols]
    wproj[...] = turned_wide(total[:, cols:])


def sum_last_body(size, *refs):
    total = total_of(refs[:size])
    wqkv, wout, vecs = refs[size:]
    width = wout.shape[0]
    for number in range(3):
        low = VEC_COLS + number * width
        wqkv[number] = total[:, low : low + width]
    wout[...] = turned_wide(total[:, VEC_COLS + 3 * width :])
    vecs[...] = turned_wide(total[:, :VEC_COLS])[:8]


def local(
    tokens,
    segments,
    grad_out,
    w_qkv,
    b_qv,
    w_out,
    b_out,
    w_fc,
    b_fc,
    w_proj,
    b_proj,
    ln1_gain,
    ln1_bias,
    ln2_gain,
    ln2_bias,
):
    size = lax.axis_size("fsdp")
    direct = size == DIRECT_SIZE
    me = lax.axis_index("fsdp")
    chunk, hidden_cols = w_fc.shape
    own_rows, width = tokens.shape
    seq_rows = segments.shape[0]
    half = 2 * own_rows
    head_cols = w_out.shape[0]
    qkv_cols = 3 * head_cols
    qv_count = b_qv.shape[1]
    place = lax.axis_index("seq") * 2 + lax.axis_index("tensor")
    scal = jnp.stack([me, place]).astype(jnp.int32)
    parts = size if direct else 1

    near = swap(tokens, "tensor")
    pair = swap(jnp.concatenate([tokens, near]), "seq")

    flat_qv = jnp.pad(b_qv.reshape(-1), (0, chunk - 2 * qv_count))
    vecs = jnp.stack([b_out, b_proj, ln1_gain, ln1_bias, ln2_gain, ln2_bias, b_fc, flat_qv])
    col = np.arange(qkv_cols)
    inner = col % head_cols
    source = (inner // qv_count) * chunk + inner % qv_count + qv_count * (col >= 2 * head_cols)
    used = (col < head_cols) | (col >= 2 * head_cols)
    row_number = lax.broadcasted_iota(jnp.int32, (width, qkv_cols), 0)
    sel = (row_number == jnp.asarray(np.where(used, source, -1), jnp.int32)[None, :]).astype(LOW)

    rows_shape = shape(8, width, F32)
    bias_shape = shape(8, qkv_cols, F32)
    wqkv_shape, wo_shape = shape(width, qkv_cols, LOW), shape(width, head_cols, LOW)
    if direct:
        (first,) = on_core(
            pack_first_body, [shape(chunk, VEC_COLS + qkv_cols + head_cols, LOW)], [], [w_qkv, w_out, vecs]
        )
        (second,) = on_core(pack_second_body, [shape(chunk, 2 * hidden_cols, LOW)], [], [w_fc, w_proj])
        firsts = pieces_of(first)
        second = after(second, *firsts[1:6])
        seconds = pieces_of(second)
    else:
        lack = jnp.zeros((chunk, VEC_COLS - 8), LOW)
        first = jnp.concatenate([vecs.T, lack, w_qkv[0], w_qkv[1], w_qkv[2], w_out.T], axis=1)
        second = jnp.concatenate([w_fc, w_proj.T], axis=1)
        firsts = [lax.all_gather(first, "fsdp", axis=0, tiled=True)]
        seconds = [lax.all_gather(second, "fsdp", axis=0, tiled=True)]
        scal = scal * jnp.asarray([0, 1], jnp.int32)
    wqkv, wo, rows, bias = on_core(
        functools.partial(open_first_body, parts),
        [wqkv_shape, wo_shape, rows_shape, bias_shape],
        [scal],
        [*firsts, sel],
        [pltpu.VMEM((width, VEC_COLS), F32)],
    )
    wo_near = swap(wo, "tensor")
    wo_pair = swap(jnp.concatenate([wo, wo_near], axis=1), "seq")

    blocks = [place ^ b for b in range(4)]
    docs = jnp.concatenate([lax.dynamic_slice_in_dim(segments, b * own_rows, own_rows, 0) for b in blocks])
    spots = jnp.concatenate([b * own_rows + jnp.arange(own_rows, dtype=jnp.int32) for b in blocks])
    marks = [docs[:, None], docs[None, :], spots[:, None], spots[None, :]]

    mask_scratch = pltpu.VMEM((seq_rows, seq_rows), F32)
    normed_scratch = pltpu.VMEM((seq_rows, width), LOW)
    qkv, mixed, lse = on_core(
        attend_body,
        [shape(seq_rows, qkv_cols, LOW), shape(seq_rows, head_cols, LOW), shape(seq_rows, 128, F32)],
        [],
        [tokens, near, pair, wqkv, bias, rows, *marks],
        [normed_scratch, mask_scratch],
        flops=2 * seq_rows * (width * qkv_cols + 2 * head_cols * seq_rows),
    )
    mixed_near = swap(mixed, "tensor")
    crossed = mixed_near.reshape(2, 2, own_rows, head_cols)[:, ::-1].reshape(seq_rows, head_cols)
    mixed_pair = swap(jnp.concatenate([mixed, crossed], axis=1), "seq")

    square = 2 * seq_rows * width * hidden_cols
    wf, wp, da, cot = on_core(
        functools.partial(open_second_body, parts),
        [
            shape(width, hidden_cols, LOW),
            shape(width, hidden_cols, LOW),
            shape(seq_rows, hidden_cols, F32),
            shape(seq_rows, width, LOW),
        ],
        [scal],
        [*seconds, grad_out],
        flops=square,
    )
    keep, send, middle, normed_two, active, grad_hidden = on_core(
        feed_body,
        [
            shape(half, width, F32),
            shape(half, width, LOW),
            shape(half, width, F32),
            shape(seq_rows, width, LOW),
            shape(seq_rows, hidden_cols, LOW),
            shape(seq_rows, hidden_cols, LOW),
        ],
        [],
        [tokens, near, pair, mixed, mixed_near, mixed_pair, wo, wo_near, wo_pair, wf, rows, da],
        flops=3 * square,
    )
    part_two = keep + swap(send, "seq").astype(F32)
    far = swap(part_two.astype(LOW), "tensor")

    piece_cols = 2 * hidden_cols
    ff_pieces = [shape(width // parts, piece_cols, F32 if step == 0 else LOW) for step in range(parts)]
    out_keep, out_send, fc_sum, *grad_ff = on_core(
        functools.partial(feed_grad_body, parts),
        [shape(half, width, F32), shape(half, width, LOW), shape(1, hidden_cols, F32), *ff_pieces],
        [scal],
        [active, wp, normed_two, grad_hidden, cot],
        [pltpu.VMEM((width, piece_cols), F32)],
        flops=3 * square,
    )
    far = after(far, fc_sum)
    grad_mid_half, grad_mid_own, early = on_core(
        middle_body,
        [shape(half, width, LOW), shape(own_rows, width, F32), rows_shape],
        [],
        [part_two, far, middle, cot, rows],
    )
    grad_mid_other = swap(grad_mid_half, "seq")

    keep_one, send_one, grad_qkv, late, qkv_sum = on_core(
        attend_back_body,
        [
            shape(half, width, F32),
            shape(half, width, LOW),
            shape(seq_rows, qkv_cols, LOW),
            rows_shape,
            bias_shape,
        ],
        [],
        [grad_mid_half, grad_mid_other, wo, wqkv, qkv, lse, tokens, near, pair, early, *marks],
        [mask_scratch],
        flops=2 * seq_rows * (width * (qkv_cols + head_cols) + 5 * head_cols * seq_rows),
    )
    part_one = keep_one + swap(send_one, "seq").astype(F32)
    late = late + swap(late, "tensor")
    late = late + swap(late, "seq")
    far_one = swap(part_one[own_rows:].astype(LOW), "tensor")
    (grad_inputs,) = on_core(
        input_body,
        [shape(own_rows, width, F32)],
        [],
        [part_one, far_one, grad_mid_own, tokens, rows],
    )

    out_half = out_keep + swap(after(out_send, grad_qkv), "seq").astype(F32)
    out_own = out_half[:own_rows] + swap(out_half[own_rows:].astype(LOW), "tensor").astype(F32)
    result = (middle[:own_rows] + out_own + rows[1:2]).astype(LOW)

    last_cols = VEC_COLS + qkv_cols + head_cols
    last_pieces = [shape(width // parts, last_cols, F32 if step == 0 else LOW) for step in range(parts)]
    grad_last = on_core(
        functools.partial(last_grad_body, parts),
        last_pieces,
        [scal],
        [
            grad_mid_half, grad_mid_other, mixed, tokens, near, pair, rows, grad_qkv, late, fc_sum, qkv_sum, sel,
        ],
        [pltpu.VMEM((width, last_cols), F32), normed_scratch],
        flops=2 * seq_rows * width * (qkv_cols + head_cols),
    )

    if direct:
        got_ff = sums_of(grad_ff)
        got_last = sums_of(grad_last)
        grad_wfc, grad_wproj = on_core(
            functools.partial(sum_feed_body, len(got_ff)),
            [shape(chunk, hidden_cols, F32), shape(hidden_cols, chunk, F32)],
            [],
            got_ff,
        )
        grad_wqkv, grad_wout, sums = on_core(
            functools.partial(sum_last_body, len(got_last)),
            [jax.ShapeDtypeStruct((3, chunk, head_cols), F32), shape(head_cols, chunk, F32), shape(8, chunk, F32)],
            [],
            got_last,
        )
    else:
        sum_ff = lax.psum_scatter(grad_ff[0], "fsdp", scatter_dimension=0, tiled=True)
        sum_last = lax.psum_scatter(grad_last[0], "fsdp", scatter_dimension=0, tiled=True)
        grad_wfc, grad_wproj = sum_ff[:, :hidden_cols], sum_ff[:, hidden_cols:].T
        split = VEC_COLS + qkv_cols
        grad_wqkv = sum_last[:, VEC_COLS:split].reshape(chunk, 3, head_cols).transpose(1, 0, 2)
        grad_wout = sum_last[:, split:].T
        sums = sum_last[:, :8].T

    return (
        result,
        grad_inputs,
        grad_wqkv,
        grad_wout,
        grad_wfc,
        grad_wproj,
        sums[7, : 2 * qv_count].reshape(2, qv_count),
        sums[0],
        sums[6],
        sums[1],
        sums[2],
        sums[3],
        sums[4],
        sums[5],
    )


def solution(mesh):
    in_specs = (
        P(("fsdp", "seq", "tensor"), None),
        P("fsdp"),
        P("fsdp", None),
        P(None, "fsdp", ("seq", "tensor")),
        P(None, ("seq", "tensor", "fsdp")),
        P(("seq", "tensor"), "fsdp"),
        P("fsdp"),
        P("fsdp", ("seq", "tensor")),
        P(("seq", "tensor", "fsdp")),
        P(("seq", "tensor"), "fsdp"),
        P("fsdp"),
        P("fsdp"),
        P("fsdp"),
        P("fsdp"),
        P("fsdp"),
    )
    out_specs = (
        P(("fsdp", "seq", "tensor"), None),
        P(("fsdp", "seq", "tensor"), None),
        P(None, "fsdp", ("seq", "tensor")),
        P(("seq", "tensor"), "fsdp"),
        P("fsdp", ("seq", "tensor")),
        P(("seq", "tensor"), "fsdp"),
        P(None, ("seq", "tensor", "fsdp")),
        P("fsdp"),
        P(("seq", "tensor", "fsdp")),
        P("fsdp"),
        P("fsdp"),
        P("fsdp"),
        P("fsdp"),
        P("fsdp"),
    )
    return jax.shard_map(local, mesh=mesh, in_specs=in_specs, out_specs=out_specs, check_vma=False)
```

```python
import functools

import jax
import jax.numpy as jnp
import numpy as np
from jax import lax
from jax.experimental import pallas as pl
from jax.experimental.pallas import tpu as pltpu
from jax.sharding import PartitionSpec as P

HEAD_DIM = 64
DIRECT_SIZE = 8
STEPS = ((0, 0), (1, 0), (3, 1), (3, 0), (1, 1), (0, 1), (2, 0), (2, 1))
VEC_COLS = 128
LOW = jnp.bfloat16
F32 = jnp.float32
GELU_SCALE = float(np.sqrt(2.0 / np.pi))


def shape(rows, cols, dtype):
    return jax.ShapeDtypeStruct((rows, cols), dtype)


def on_core(body, outs, scalars, arrays, scratch=(), flops=0, limit=40):
    specs = [pl.BlockSpec(memory_space=pltpu.SMEM)] * len(scalars)
    specs += [pl.BlockSpec()] * len(arrays)
    moved = sum(int(np.prod(a.shape)) * a.dtype.itemsize for a in arrays) + sum(
        int(np.prod(o.shape)) * o.dtype.itemsize for o in outs
    )
    return pl.pallas_call(
        body,
        out_shape=tuple(outs),
        in_specs=specs,
        out_specs=tuple(pl.BlockSpec() for _ in outs),
        scratch_shapes=list(scratch),
        compiler_params=pltpu.CompilerParams(vmem_limit_bytes=limit * 2**20),
        cost_estimate=pl.CostEstimate(flops=flops, bytes_accessed=moved, transcendentals=0),
    )(*scalars, *arrays)


def dot(left, right, left_dim, right_dim):
    return lax.dot_general(
        left, right, (((left_dim,), (right_dim,)), ((), ())), preferred_element_type=F32
    )


def norm_parts(values):
    center = values - jnp.mean(values, axis=-1, keepdims=True)
    spread = jnp.mean(center * center, axis=-1, keepdims=True)
    inverse = lax.rsqrt(spread + 1e-05)
    return center * inverse, inverse


def norm_back(cot, scaled, inverse, gain):
    inner = cot * gain
    first = jnp.mean(inner, axis=-1, keepdims=True)
    second = jnp.mean(inner * scaled, axis=-1, keepdims=True)
    return (inner - first - scaled * second) * inverse


def turned(value):
    count = value.shape[1]
    row = lax.broadcasted_iota(jnp.int32, (count, count), 0)
    col = lax.broadcasted_iota(jnp.int32, (count, count), 1)
    return dot((row == col).astype(F32).astype(LOW), value, 1, 1).astype(LOW)


def turned_wide(value):
    rows = value.shape[0]
    lack = -rows % 128
    if lack:
        value = jnp.concatenate([value, jnp.zeros((lack, value.shape[1]), value.dtype)], axis=0)
    return value.T[:, :rows]


def swap(value, axis):
    return lax.ppermute(value, axis, [(0, 1), (1, 0)])


def send(value, turn, flip):
    pairs = [(i, (i // 2 + turn) % 4 * 2 + (i % 2 ^ flip)) for i in range(DIRECT_SIZE)]
    return lax.ppermute(value, "fsdp", pairs)


def after(value, *earlier):
    return lax.optimization_barrier((value, *earlier))[0]


def pieces_ring_first(chunk):
    ahead, behind = send(chunk, 3, 0), send(chunk, 1, 0)
    other = send(chunk, 0, 1)
    far = send(ahead, 3, 0)
    across = [send(behind, 0, 1), send(ahead, 0, 1)]
    return [chunk, ahead, across[0], behind, across[1], other, far, send(far, 0, 1)]


def pieces_mixed(chunk, ring_free, pair_free):
    ahead, behind = [send(after(chunk, ring_free), turn, 0) for turn in (3, 1)]
    other = send(after(chunk, *pair_free), 0, 1)
    far = send(ahead, 3, 0)
    return [chunk, ahead, send(other, 1, 0), behind, send(ahead, 0, 1), other, far, send(far, 0, 1)]


def added(*values):
    total = values[0].astype(F32)
    for value in values[1:]:
        total = total + value.astype(F32)
    return total.astype(LOW)


def over_pair(pieces):
    return [send(pieces[step], 0, 1) for step in (7, 4, 2, 5)]


def round_ring(pieces, got):
    far = send(added(pieces[6], got[0]), 1, 0)
    behind = send(added(pieces[3], got[2]), 3, 0)
    ahead = send(added(pieces[1], got[1], far), 1, 0)
    return [pieces[0], got[3], ahead, behind]


def row_start(me, step, rows):
    turn, flip = STEPS[step]
    pair = lax.rem(lax.div(me, 2) + turn, 4)
    return pl.multiple_of((pair * 2 + (lax.rem(me, 2) ^ flip)) * rows, rows)


def pack_body(wqkv, wout, wfc, wproj, bqv, *refs):
    vecs, first, second = refs[:-2], refs[-2], refs[-1]
    rows = wqkv.shape[1]
    lines = [vec[...].astype(F32).reshape(1, rows) for vec in vecs]
    lack = jnp.zeros((2, rows - bqv.shape[1]), F32)
    lines.append(jnp.concatenate([bqv[...].astype(F32), lack], axis=1))
    lines.append(jnp.zeros((VEC_COLS - len(vecs) - 2, rows), F32))
    cols = jnp.concatenate(lines, axis=0)
    lack = -rows % 128
    if lack:
        cols = jnp.concatenate([cols, jnp.zeros((VEC_COLS, lack), F32)], axis=1)
    cols = cols.T[:rows].astype(LOW)
    first[...] = jnp.concatenate([cols, wqkv[0], wqkv[1], wqkv[2], turned(wout[...])], axis=1)
    second[...] = jnp.concatenate([wfc[...], wproj[...]], axis=1)


def open_first_body(size, scal, *refs):
    pieces, (sel, wqkv, wo, rows, bias, cols) = refs[:size], refs[size:]
    chunk = pieces[0].shape[0]
    split = VEC_COLS + wqkv.shape[1]
    end = split + wo.shape[1]
    for step, piece in enumerate(pieces):
        place = pl.ds(row_start(scal[0], step, chunk) if size > 1 else 0, chunk)
        value = piece[:, :end]
        cols[place, :] = value[:, :VEC_COLS].astype(F32)
        wqkv[place, :] = value[:, VEC_COLS:split]
        wo[place, :] = value[:, split:]
    wide = cols[...].T
    rows[...] = wide[:8]
    spread = dot(wide[:16].astype(LOW), sel[...], 1, 0)
    col = lax.broadcasted_iota(jnp.int32, (8, bias.shape[1]), 1)
    count = wo.shape[1]
    bias[...] = jnp.where(col < count, spread[7:8], jnp.where(col >= 2 * count, spread[8:9], 0.0))


def open_second_body(size, scal, *refs):
    pieces, (grad, wf, wp, da, cot) = refs[:size], refs[size:]
    chunk = pieces[-1].shape[0]
    cols = wf.shape[1]
    own = cot.shape[0] // 4
    for step, piece in enumerate(pieces):
        place = pl.ds(row_start(scal[0], step, chunk) if size > 1 else 0, chunk)
        wf[place, :] = piece[:, :cols]
        wp[place, :] = piece[:, cols:]
    for block in range(4):
        start = pl.multiple_of((scal[1] ^ block) * own, own)
        cot[block * own : (block + 1) * own, :] = grad[pl.ds(start, own), :]
    da[...] = dot(cot[...], wp[...], 1, 0)


def fill_mask(mask, doc_col, doc_row, pos_col, pos_row):
    total = mask.shape[0]
    for low in range(0, total, 128):
        part = slice(low, low + 128)
        seen = (doc_col[part, :] == doc_row[...]) & (pos_row[...] <= pos_col[part, :])
        mask[part, :] = jnp.where(seen, 0.0, -1e30)


def attend_body(
    tok0, tok1, tok2, tok3, wqkv, bias, rows, doc_col, doc_row, pos_col, pos_row,
    qkv, mixed, lse, normed, mask,
):
    total = qkv.shape[0]
    part = tok0.shape[0]
    gain, shift = rows[2:3, :], rows[3:4, :]
    for number, source in enumerate((tok0, tok1, tok2, tok3)):
        scaled, _ = norm_parts(source[...].astype(F32))
        normed[number * part : (number + 1) * part, :] = (scaled * gain + shift).astype(LOW)
    qkv[...] = (dot(normed[...], wqkv[...], 1, 0) + bias[7:8, :]).astype(LOW)
    fill_mask(mask, doc_col, doc_row, pos_col, pos_row)
    width = qkv.shape[1] // 3
    heads = width // HEAD_DIM
    step = total // 2
    for low in range(0, total, step):
        here = slice(low, low + step)
        found, norms = [], []
        for head in range(heads):
            at = head * HEAD_DIM
            query = qkv[here, at : at + HEAD_DIM]
            key = qkv[:, width + at : width + at + HEAD_DIM]
            value = qkv[:, 2 * width + at : 2 * width + at + HEAD_DIM]
            scores = dot(query, key, 1, 1) * 0.125 + mask[here, :]
            top = jnp.max(scores, axis=-1, keepdims=True)
            raised = jnp.exp(scores - top)
            total_raised = jnp.sum(raised, axis=-1, keepdims=True)
            probs = (raised * (1.0 / total_raised)).astype(LOW)
            found.append(dot(probs, value, 1, 0))
            norms.append(top + jnp.log(total_raised))
        mixed[here, :] = jnp.concatenate(found, axis=1).astype(LOW)
        for head in range(heads):
            lse[here, head : head + 1] = norms[head]


def feed_body(
    tok0, tok1, tok2, tok3, mixed0, mixed1, mixed2, mixed3, wo0, wo1, wo2, wo3, wf, rows, da,
    keep, send, middle, normed, active, grad_hidden,
):
    part = tok0.shape[0]
    half = 2 * part
    toks = (tok0, tok1, tok2, tok3)
    for number in range(2):
        here = slice(number * half, (number + 1) * half)
        source = jnp.concatenate([toks[2 * number][...], toks[2 * number + 1][...]], axis=0)
        total = source.astype(F32) + rows[0:1, :]
        for peer, (found, weight) in enumerate(((mixed0, wo0), (mixed1, wo1), (mixed2, wo2), (mixed3, wo3))):
            blocks = [found[(b ^ peer) * part : (b ^ peer) * part + part, :] for b in (2 * number, 2 * number + 1)]
            total += dot(jnp.concatenate(blocks, axis=0), weight[...], 1, 1)
        if number == 0:
            middle[...] = total
        scaled, _ = norm_parts(total)
        low_norm = (scaled * rows[4:5, :] + rows[5:6, :]).astype(LOW)
        normed[here, :] = low_norm
        hidden = dot(low_norm, wf[...], 1, 0) + rows[6:7, :]
        square = hidden * hidden
        bent = jnp.tanh(GELU_SCALE * hidden * (1.0 + 0.044715 * square))
        rise = 0.5 * (1.0 + bent)
        active[here, :] = (hidden * rise).astype(LOW)
        slope = rise + 0.5 * hidden * (1.0 - bent * bent) * (
            GELU_SCALE * (1.0 + 3 * 0.044715 * square)
        )
        grad_low = (da[here, :] * slope).astype(LOW)
        grad_hidden[here, :] = grad_low
        back = dot(grad_low, wf[...], 1, 1)
        if number == 0:
            keep[...] = back
        else:
            send[...] = back.astype(LOW)


def put_pieces(me, outs, parts):
    chunk = outs[0].shape[0]
    for step, out in enumerate(outs):
        place = pl.ds(row_start(me, step, chunk), chunk) if len(outs) > 1 else slice(None)
        low = 0
        for part in parts:
            high = low + part.shape[1]
            out[:, low:high] = part[place, :].astype(out.dtype)
            low = high


def piece_shapes(parts, width, cols):
    return [shape(width // parts, cols, LOW if step else F32) for step in range(parts)]


def feed_grad_body(scal, active, wp, normed, grad_hidden, cot, *refs):
    keep, send, fc_sum = refs[:3]
    pieces, whole = refs[3:-1], refs[-1]
    half = keep.shape[0]
    cols = wp.shape[1]
    whole[:, :cols] = dot(normed[...], grad_hidden[...], 0, 0)
    whole[:, cols:] = dot(cot[...], active[...], 0, 0)
    put_pieces(scal[0], pieces, [whole])
    keep[...] = dot(active[:half, :], wp[...], 1, 1)
    send[...] = dot(active[half:, :], wp[...], 1, 1).astype(LOW)
    fc_sum[...] = jnp.sum(grad_hidden[...].astype(F32), axis=0, keepdims=True)


def middle_body(part_two, far, middle, cot, rows, grad_low, grad_own, early):
    own = grad_own.shape[0]
    flipped = jnp.concatenate([far[own:, :], far[:own, :]], axis=0).astype(F32)
    grad = part_two[...] + flipped
    scaled, inverse = norm_parts(middle[...])
    cotangent = cot[: 2 * own, :].astype(F32)
    total = cotangent + norm_back(grad, scaled, inverse, rows[4:5, :])
    grad_low[...] = total.astype(LOW)
    grad_own[...] = total[:own]
    add = functools.partial(jnp.sum, axis=0, keepdims=True)
    empty = jnp.zeros((2, total.shape[1]), F32)
    early[...] = jnp.concatenate(
        [add(total[:own]), add(cotangent[:own]), empty, add(grad[:own] * scaled[:own]), add(grad[:own]), empty],
        axis=0,
    )


def attend_back_body(
    grad_half, grad_other, wo, wqkv, qkv, lse, tok0, tok1, tok2, tok3, early, doc_col, doc_row, pos_col, pos_row,
    keep, send, grad_qkv, late, qkv_sum, mask,
):
    total = qkv.shape[0]
    half = total // 2
    toks = (tok0, tok1, tok2, tok3)
    width = qkv.shape[1] // 3
    heads = width // HEAD_DIM
    fill_mask(mask, doc_col, doc_row, pos_col, pos_row)
    grad_attn = [dot(g[...], wo[...], 1, 0).astype(LOW) for g in (grad_half, grad_other)]
    query_grads = [[], []]
    key_grads, value_grads = [], []
    for head in range(heads):
        at = head * HEAD_DIM
        key = qkv[:, width + at : width + at + HEAD_DIM]
        value = qkv[:, 2 * width + at : 2 * width + at + HEAD_DIM]
        key_grad = value_grad = None
        for number in range(2):
            here = slice(number * half, (number + 1) * half)
            query = qkv[here, at : at + HEAD_DIM]
            grad = grad_attn[number][:, at : at + HEAD_DIM]
            scores = dot(query, key, 1, 1) * 0.125 + mask[here, :]
            probs = jnp.exp(scores - lse[here, head : head + 1])
            grad_probs = dot(grad, value, 1, 1)
            inner = jnp.sum(probs * grad_probs, axis=-1, keepdims=True)
            grad_scores = (probs * (grad_probs - inner)).astype(LOW)
            query_grads[number].append(dot(grad_scores, key, 1, 0) * 0.125)
            more_key = dot(grad_scores, query, 0, 0)
            more_value = dot(probs.astype(LOW), grad, 0, 0)
            key_grad = more_key if key_grad is None else key_grad + more_key
            value_grad = more_value if value_grad is None else value_grad + more_value
        key_grads.append(key_grad * 0.125)
        value_grads.append(value_grad)
    for number in range(2):
        here = slice(number * half, (number + 1) * half)
        grad_qkv[here, :] = jnp.concatenate(
            query_grads[number] + [k[here] for k in key_grads] + [v[here] for v in value_grads], axis=1
        ).astype(LOW)
    gain_sum = shift_sum = 0.0
    for number in range(2):
        here = slice(number * half, (number + 1) * half)
        back = dot(grad_qkv[here, :], wqkv[...], 1, 1)
        source = jnp.concatenate([toks[2 * number][...], toks[2 * number + 1][...]], axis=0)
        scaled, _ = norm_parts(source.astype(F32))
        gain_sum += jnp.sum(back * scaled, axis=0, keepdims=True)
        shift_sum += jnp.sum(back, axis=0, keepdims=True)
        if number == 0:
            keep[...] = back
        else:
            send[...] = back.astype(LOW)
    late[...] = jnp.concatenate([early[:2, :], gain_sum, shift_sum, early[4:, :]], axis=0)
    sums = jnp.sum(grad_qkv[...].astype(F32), axis=0, keepdims=True)
    qkv_sum[...] = jnp.concatenate([sums, jnp.zeros((7, sums.shape[1]), F32)], axis=0)


def last_grad_body(
    grad_half, grad_other, mixed, tok0, tok1, tok2, tok3, rows, grad_qkv, fc_sum, qkv_sum, sel, whole, lines, normed
):
    part = tok0.shape[0]
    half = 2 * part
    for number, source in enumerate((tok0, tok1, tok2, tok3)):
        scaled, _ = norm_parts(source[...].astype(F32))
        normed[number * part : (number + 1) * part, :] = (scaled * rows[2:3, :] + rows[3:4, :]).astype(LOW)
    split = grad_qkv.shape[1]
    whole[:, :split] = dot(normed[...], grad_qkv[...], 0, 0)
    whole[:, split:] = dot(grad_half[...], mixed[:half, :], 0, 0) + dot(grad_other[...], mixed[half:, :], 0, 0)
    count = qkv_sum.shape[1] // 3
    col = lax.broadcasted_iota(jnp.int32, qkv_sum.shape, 1)
    line = lax.broadcasted_iota(jnp.int32, qkv_sum.shape, 0)
    sums = qkv_sum[0:1, :]
    sums = jnp.where((line == 0) & (col < count) | (line == 1) & (col >= 2 * count), sums, 0.0)
    placed = lax.dot_general(
        sums, sel[...].astype(F32), (((1,), (1,)), ((), ())),
        preferred_element_type=F32, precision=lax.Precision.HIGHEST,
    )
    lines[...] = jnp.concatenate([fc_sum[...], placed[:7]], axis=0)


def last_cut_body(scal, whole, late, lines, *refs):
    pieces, cols = refs[:-1], refs[-1]
    line = jnp.concatenate([late[:6, :], lines[:3, :]], axis=0)
    lack = jnp.zeros((VEC_COLS - line.shape[0], line.shape[1]), F32)
    cols[...] = jnp.concatenate([line, lack], axis=0).T
    put_pieces(scal[0], pieces, [cols, whole])


def input_body(keep, far, middle_grad, own, rows, out):
    part = own.shape[0]
    grad = keep[:part, :] + far[...].astype(F32)
    scaled, inverse = norm_parts(own[...].astype(F32))
    out[...] = middle_grad[...] + norm_back(grad, scaled, inverse, rows[2:3, :])


def total_of(*refs):
    total = refs[0][...]
    for ref in refs[1:]:
        total = total + ref[...].astype(F32)
    return total


def sum_feed_body(*refs):
    total = total_of(*refs[:4])
    wfc, wproj = refs[4:]
    cols = wfc.shape[1]
    wfc[...] = total[:, :cols]
    wproj[...] = total[:, cols:]


def sum_last_body(*refs):
    total = total_of(*refs[:4])
    wqkv, wout, vecs = refs[4:]
    width = wout.shape[0]
    for number in range(3):
        low = VEC_COLS + number * width
        wqkv[number] = total[:, low : low + width]
    wout[...] = turned_wide(total[:, VEC_COLS + 3 * width :])
    vecs[...] = turned_wide(total[:, :VEC_COLS])[:16]


def local(
    tokens,
    segments,
    grad_out,
    w_qkv,
    b_qv,
    w_out,
    b_out,
    w_fc,
    b_fc,
    w_proj,
    b_proj,
    ln1_gain,
    ln1_bias,
    ln2_gain,
    ln2_bias,
):
    size = lax.axis_size("fsdp")
    direct = size == DIRECT_SIZE
    me = lax.axis_index("fsdp")
    chunk, hidden_cols = w_fc.shape
    own_rows, width = tokens.shape
    seq_rows = segments.shape[0]
    half = 2 * own_rows
    head_cols = w_out.shape[0]
    qkv_cols = 3 * head_cols
    qv_count = b_qv.shape[1]
    place = lax.axis_index("seq") * 2 + lax.axis_index("tensor")
    scal = jnp.stack([me, place]).astype(jnp.int32)
    parts = size if direct else 1

    near = swap(tokens, "tensor")
    toks = [tokens, near, swap(tokens, "seq"), swap(near, "seq")]

    vecs = [b_out, b_proj, ln1_gain, ln1_bias, ln2_gain, ln2_bias, b_fc]
    col = np.arange(qkv_cols)
    inner = col % head_cols
    source = (inner // qv_count) * chunk + inner % qv_count
    row_number = lax.broadcasted_iota(jnp.int32, (width, qkv_cols), 0)
    sel = (row_number == jnp.asarray(source, jnp.int32)[None, :]).astype(LOW)

    rows_shape = shape(8, width, F32)
    bias_shape = shape(8, qkv_cols, F32)
    wqkv_shape, wo_shape = shape(width, qkv_cols, LOW), shape(width, head_cols, LOW)
    if direct:
        first, second = on_core(
            pack_body,
            [shape(chunk, VEC_COLS + qkv_cols + head_cols, LOW), shape(chunk, 2 * hidden_cols, LOW)],
            [],
            [w_qkv, w_out, w_fc, w_proj.T, b_qv, *vecs],
            limit=62,
        )
        firsts = pieces_ring_first(first)
        seconds = pieces_mixed(second, firsts[6], [firsts[2], firsts[4]])
    else:
        lines = jnp.stack([*vecs, *jnp.pad(b_qv, ((0, 0), (0, chunk - qv_count)))])
        lack = jnp.zeros((chunk, VEC_COLS - lines.shape[0]), LOW)
        first = jnp.concatenate([lines.T, lack, w_qkv[0], w_qkv[1], w_qkv[2], w_out.T], axis=1)
        second = jnp.concatenate([w_fc, w_proj.T], axis=1)
        firsts = [lax.all_gather(first, "fsdp", axis=0, tiled=True)]
        seconds = [lax.all_gather(second, "fsdp", axis=0, tiled=True)]
        scal = scal * jnp.asarray([0, 1], jnp.int32)
    wqkv, wo, rows, bias = on_core(
        functools.partial(open_first_body, parts),
        [wqkv_shape, wo_shape, rows_shape, bias_shape],
        [scal],
        [*firsts, sel],
        [pltpu.VMEM((width, VEC_COLS), F32)],
    )
    wo_near = swap(wo, "tensor")
    wos = [wo, wo_near, swap(wo, "seq"), swap(wo_near, "seq")]

    blocks = [place ^ b for b in range(4)]
    docs = jnp.concatenate([lax.dynamic_slice_in_dim(segments, b * own_rows, own_rows, 0) for b in blocks])
    spots = jnp.concatenate([b * own_rows + jnp.arange(own_rows, dtype=jnp.int32) for b in blocks])
    marks = [docs[:, None], docs[None, :], spots[:, None], spots[None, :]]

    mask_scratch = pltpu.VMEM((seq_rows, seq_rows), F32)
    normed_scratch = pltpu.VMEM((seq_rows, width), LOW)
    qkv, mixed, lse = on_core(
        attend_body,
        [shape(seq_rows, qkv_cols, LOW), shape(seq_rows, head_cols, LOW), shape(seq_rows, 128, F32)],
        [],
        [*toks, wqkv, bias, rows, *marks],
        [normed_scratch, mask_scratch],
        flops=2 * seq_rows * (width * qkv_cols + 2 * head_cols * seq_rows),
    )
    mixed_near = swap(mixed, "tensor")
    mixeds = [mixed, mixed_near, swap(mixed, "seq"), swap(mixed_near, "seq")]

    square = 2 * seq_rows * width * hidden_cols
    wf, wp, da, cot = on_core(
        functools.partial(open_second_body, parts),
        [
            shape(width, hidden_cols, LOW),
            shape(width, hidden_cols, LOW),
            shape(seq_rows, hidden_cols, F32),
            shape(seq_rows, width, LOW),
        ],
        [scal],
        [*seconds, grad_out],
        flops=square,
    )
    keep, send, middle, normed_two, active, grad_hidden = on_core(
        feed_body,
        [
            shape(half, width, F32),
            shape(half, width, LOW),
            shape(half, width, F32),
            shape(seq_rows, width, LOW),
            shape(seq_rows, hidden_cols, LOW),
            shape(seq_rows, hidden_cols, LOW),
        ],
        [],
        [*toks, *mixeds, *wos, wf, rows, da],
        flops=3 * square,
    )
    part_two = keep + swap(send, "seq").astype(F32)
    far = swap(part_two.astype(LOW), "tensor")

    piece_cols = 2 * hidden_cols
    out_keep, out_send, fc_sum, *grad_ff = on_core(
        feed_grad_body,
        [shape(half, width, F32), shape(half, width, LOW), shape(1, hidden_cols, F32), *piece_shapes(parts, width, piece_cols)],
        [scal],
        [active, wp, normed_two, grad_hidden, after(cot, part_two)],
        [pltpu.VMEM((width, piece_cols), F32)],
        flops=3 * square,
    )
    out_half = out_keep + swap(out_send, "seq").astype(F32)
    out_far = swap(out_half[own_rows:].astype(LOW), "tensor")
    result = (middle[:own_rows] + out_half[:own_rows] + out_far.astype(F32) + rows[1:2]).astype(LOW)
    far = after(far, fc_sum, out_half)
    if direct:
        crossed = over_pair(grad_ff)
        far = after(far, crossed[0])
    grad_mid_half, grad_mid_own, early = on_core(
        middle_body,
        [shape(half, width, LOW), shape(own_rows, width, F32), rows_shape],
        [],
        [part_two, far, middle, cot, rows],
    )
    grad_mid_other = swap(grad_mid_half, "seq")

    if direct:
        grad_mid_other = after(grad_mid_other, crossed[1])
        got_ff = round_ring(grad_ff, crossed)
    keep_one, send_one, grad_qkv, late, qkv_sum = on_core(
        attend_back_body,
        [
            shape(half, width, F32),
            shape(half, width, LOW),
            shape(seq_rows, qkv_cols, LOW),
            rows_shape,
            bias_shape,
        ],
        [],
        [grad_mid_half, grad_mid_other, wo, wqkv, qkv, lse, *toks, early, *marks],
        [mask_scratch],
        flops=2 * seq_rows * (width * (qkv_cols + head_cols) + 5 * head_cols * seq_rows),
    )
    part_one = keep_one + swap(send_one, "seq").astype(F32)
    late = late + swap(late, "tensor")
    late = late + swap(late, "seq")
    far_one = swap(part_one[own_rows:].astype(LOW), "tensor")
    (grad_inputs,) = on_core(
        input_body,
        [shape(own_rows, width, F32)],
        [],
        [part_one, far_one, grad_mid_own, tokens, rows],
    )

    last_cols = VEC_COLS + qkv_cols + head_cols
    whole, lines = on_core(
        last_grad_body,
        [shape(width, qkv_cols + head_cols, F32), rows_shape],
        [],
        [grad_mid_half, grad_mid_other, mixed, *toks, rows, grad_qkv, fc_sum, qkv_sum, sel],
        [normed_scratch],
        flops=2 * seq_rows * width * (qkv_cols + head_cols),
    )
    late = after(late, part_one)
    if direct:
        late = after(late, *crossed)
    grad_last = on_core(
        last_cut_body,
        piece_shapes(parts, width, last_cols),
        [scal],
        [whole, late, lines],
        [pltpu.VMEM((width, VEC_COLS), F32)],
    )

    if direct:
        crossed = over_pair(grad_last)
        crossed[2] = after(crossed[2], far_one, out_far)
        got_last = round_ring(grad_last, crossed)
        grad_wfc, grad_wproj = on_core(
            sum_feed_body,
            [shape(chunk, hidden_cols, F32)] * 2,
            [],
            got_ff,
        )
        grad_wproj = grad_wproj.T
        grad_wqkv, grad_wout, sums = on_core(
            sum_last_body,
            [jax.ShapeDtypeStruct((3, chunk, head_cols), F32), shape(head_cols, chunk, F32), shape(16, chunk, F32)],
            [],
            got_last,
        )
    else:
        sum_ff = lax.psum_scatter(grad_ff[0], "fsdp", scatter_dimension=0, tiled=True)
        sum_last = lax.psum_scatter(grad_last[0], "fsdp", scatter_dimension=0, tiled=True)
        grad_wfc, grad_wproj = sum_ff[:, :hidden_cols], sum_ff[:, hidden_cols:].T
        split = VEC_COLS + qkv_cols
        grad_wqkv = sum_last[:, VEC_COLS:split].reshape(chunk, 3, head_cols).transpose(1, 0, 2)
        grad_wout = sum_last[:, split:].T
        sums = sum_last[:, :16].T

    return (
        result,
        grad_inputs,
        grad_wqkv,
        grad_wout,
        grad_wfc,
        grad_wproj,
        sums[7:9, :qv_count],
        sums[0],
        sums[6],
        sums[1],
        sums[2],
        sums[3],
        sums[4],
        sums[5],
    )


def solution(mesh):
    in_specs = (
        P(("fsdp", "seq", "tensor"), None),
        P("fsdp"),
        P("fsdp", None),
        P(None, "fsdp", ("seq", "tensor")),
        P(None, ("seq", "tensor", "fsdp")),
        P(("seq", "tensor"), "fsdp"),
        P("fsdp"),
        P("fsdp", ("seq", "tensor")),
        P(("seq", "tensor", "fsdp")),
        P(("seq", "tensor"), "fsdp"),
        P("fsdp"),
        P("fsdp"),
        P("fsdp"),
        P("fsdp"),
        P("fsdp"),
    )
    out_specs = (
        P(("fsdp", "seq", "tensor"), None),
        P(("fsdp", "seq", "tensor"), None),
        P(None, "fsdp", ("seq", "tensor")),
        P(("seq", "tensor"), "fsdp"),
        P("fsdp", ("seq", "tensor")),
        P(("seq", "tensor"), "fsdp"),
        P(None, ("seq", "tensor", "fsdp")),
        P("fsdp"),
        P(("seq", "tensor", "fsdp")),
        P("fsdp"),
        P("fsdp"),
        P("fsdp"),
        P("fsdp"),
        P("fsdp"),
    )
    return jax.shard_map(local, mesh=mesh, in_specs=in_specs, out_specs=out_specs, check_vma=False)
```

```python
import functools

import jax
import jax.numpy as jnp
import numpy as np
from jax import lax
from jax.experimental import pallas as pl
from jax.experimental.pallas import tpu as pltpu
from jax.sharding import PartitionSpec as P

HEAD_DIM = 64
DIRECT_SIZE = 8
STEPS = ((0, 0), (1, 0), (3, 1), (3, 0), (1, 1), (0, 1), (2, 0), (2, 1))
VEC_COLS = 128
FIRST_LIMIT = 40
LOW = jnp.bfloat16
F32 = jnp.float32
GELU_SCALE = float(np.sqrt(2.0 / np.pi))


def shape(rows, cols, dtype):
    return jax.ShapeDtypeStruct((rows, cols), dtype)


def on_core(body, outs, scalars, arrays, scratch=(), flops=0, limit=40):
    specs = [pl.BlockSpec(memory_space=pltpu.SMEM)] * len(scalars)
    specs += [pl.BlockSpec()] * len(arrays)
    moved = sum(int(np.prod(a.shape)) * a.dtype.itemsize for a in arrays) + sum(
        int(np.prod(o.shape)) * o.dtype.itemsize for o in outs
    )
    return pl.pallas_call(
        body,
        out_shape=tuple(outs),
        in_specs=specs,
        out_specs=tuple(pl.BlockSpec() for _ in outs),
        scratch_shapes=list(scratch),
        compiler_params=pltpu.CompilerParams(vmem_limit_bytes=limit * 2**20),
        cost_estimate=pl.CostEstimate(flops=flops, bytes_accessed=moved, transcendentals=0),
    )(*scalars, *arrays)


def dot(left, right, left_dim, right_dim):
    return lax.dot_general(
        left, right, (((left_dim,), (right_dim,)), ((), ())), preferred_element_type=F32
    )


def norm_parts(values):
    center = values - jnp.mean(values, axis=-1, keepdims=True)
    spread = jnp.mean(center * center, axis=-1, keepdims=True)
    inverse = lax.rsqrt(spread + 1e-05)
    return center * inverse, inverse


def norm_back(cot, scaled, inverse, gain):
    inner = cot * gain
    first = jnp.mean(inner, axis=-1, keepdims=True)
    second = jnp.mean(inner * scaled, axis=-1, keepdims=True)
    return (inner - first - scaled * second) * inverse


def turned(value):
    count = value.shape[1]
    row = lax.broadcasted_iota(jnp.int32, (count, count), 0)
    col = lax.broadcasted_iota(jnp.int32, (count, count), 1)
    return dot((row == col).astype(F32).astype(LOW), value, 1, 1).astype(LOW)


def turned_wide(value):
    rows = value.shape[0]
    lack = -rows % 128
    if lack:
        value = jnp.concatenate([value, jnp.zeros((lack, value.shape[1]), value.dtype)], axis=0)
    return value.T[:, :rows]


def swap(value, axis):
    return lax.ppermute(value, axis, [(0, 1), (1, 0)])


def send(value, turn, flip):
    pairs = [(i, (i // 2 + turn) % 4 * 2 + (i % 2 ^ flip)) for i in range(DIRECT_SIZE)]
    return lax.ppermute(value, "fsdp", pairs)


def after(value, *earlier):
    return lax.optimization_barrier((value, *earlier))[0]


def pieces_ring_first(chunk):
    ahead, behind = send(chunk, 3, 0), send(chunk, 1, 0)
    other = send(chunk, 0, 1)
    far = send(ahead, 3, 0)
    across = [send(behind, 0, 1), send(ahead, 0, 1)]
    return [chunk, ahead, across[0], behind, across[1], other, far, send(far, 0, 1)]


def pieces_mixed(chunk, ring_free):
    ahead, behind = [send(after(chunk, *ring_free), turn, 0) for turn in (3, 1)]
    other = send(chunk, 0, 1)
    far = send(ahead, 3, 0)
    return [chunk, ahead, send(other, 1, 0), behind, send(ahead, 0, 1), other, far, send(far, 0, 1)]


def added(*values):
    total = values[0].astype(F32)
    for value in values[1:]:
        total = total + value.astype(F32)
    return total.astype(LOW)


def sums_begin(pieces):
    return [send(pieces[7], 0, 1), send(pieces[4], 0, 1), send(pieces[2], 3, 0), send(pieces[3], 3, 0)]


def sums_end(pieces, got):
    far = send(added(after(pieces[6], got[2]), got[0]), 1, 0)
    other = send(added(after(pieces[5], far), got[2]), 0, 1)
    ahead = send(added(pieces[1], got[1], far), 1, 0)
    return [pieces[0], got[3], other, ahead]


def row_start(me, step, rows):
    turn, flip = STEPS[step]
    pair = lax.rem(lax.div(me, 2) + turn, 4)
    return pl.multiple_of((pair * 2 + (lax.rem(me, 2) ^ flip)) * rows, rows)


def pack_body(wqkv, wout, wfc, wproj, bqv, *refs):
    vecs, first, second = refs[:-2], refs[-2], refs[-1]
    rows = wqkv.shape[1]
    lines = [vec[...].astype(F32).reshape(1, rows) for vec in vecs]
    lack = jnp.zeros((2, rows - bqv.shape[1]), F32)
    lines.append(jnp.concatenate([bqv[...].astype(F32), lack], axis=1))
    lines.append(jnp.zeros((VEC_COLS - len(vecs) - 2, rows), F32))
    cols = jnp.concatenate(lines, axis=0)
    lack = -rows % 128
    if lack:
        cols = jnp.concatenate([cols, jnp.zeros((VEC_COLS, lack), F32)], axis=1)
    cols = cols.T[:rows].astype(LOW)
    first[...] = jnp.concatenate([cols, wqkv[0], wqkv[1], wqkv[2], turned(wout[...])], axis=1)
    second[...] = jnp.concatenate([wfc[...], wproj[...]], axis=1)


def open_second_body(size, scal, *refs):
    pieces, (grad, wf, wp, da, cot) = refs[:size], refs[size:]
    chunk = pieces[-1].shape[0]
    cols = wf.shape[1]
    own = cot.shape[0] // 4
    for step, piece in enumerate(pieces):
        place = pl.ds(row_start(scal[0], step, chunk) if size > 1 else 0, chunk)
        wf[place, :] = piece[:, :cols]
        wp[place, :] = piece[:, cols:]
    for block in range(4):
        start = pl.multiple_of((scal[1] ^ block) * own, own)
        cot[block * own : (block + 1) * own, :] = grad[pl.ds(start, own), :]
    da[...] = dot(cot[...], wp[...], 1, 0)


def fill_mask(mask, doc_col, doc_row, pos_col, pos_row):
    total = mask.shape[0]
    for low in range(0, total, 128):
        part = slice(low, low + 128)
        seen = (doc_col[part, :] == doc_row[...]) & (pos_row[...] <= pos_col[part, :])
        mask[part, :] = jnp.where(seen, 0.0, -1e30)


def attend_body(size, scal, *refs):
    pieces, refs = refs[:size], refs[size:]
    sel, tok0, tok1, tok2, tok3, doc_col, doc_row, pos_col, pos_row = refs[:9]
    qkv, mixed, lse, wqkv, wo, rows, cols, normed, mask = refs[9:]
    chunk = pieces[0].shape[0]
    split = VEC_COLS + wqkv.shape[1]
    end = split + wo.shape[1]
    for step, piece in enumerate(pieces):
        place = pl.ds(row_start(scal[0], step, chunk) if size > 1 else 0, chunk)
        value = piece[:, :end]
        cols[place, :] = value[:, :VEC_COLS].astype(F32)
        wqkv[place, :] = value[:, VEC_COLS:split]
        wo[place, :] = value[:, split:]
    wide = cols[...].T
    rows[...] = wide[:8]
    spread = dot(wide[:16].astype(LOW), sel[...], 1, 0)
    col = lax.broadcasted_iota(jnp.int32, (1, qkv.shape[1]), 1)
    count = wo.shape[1]
    bias = jnp.where(col < count, spread[7:8], jnp.where(col >= 2 * count, spread[8:9], 0.0))
    total = qkv.shape[0]
    part = tok0.shape[0]
    gain, shift = wide[2:3], wide[3:4]
    for number, source in enumerate((tok0, tok1, tok2, tok3)):
        scaled, _ = norm_parts(source[...].astype(F32))
        normed[number * part : (number + 1) * part, :] = (scaled * gain + shift).astype(LOW)
    qkv[...] = (dot(normed[...], wqkv[...], 1, 0) + bias).astype(LOW)
    fill_mask(mask, doc_col, doc_row, pos_col, pos_row)
    width = qkv.shape[1] // 3
    heads = width // HEAD_DIM
    step = total // 2
    for low in range(0, total, step):
        here = slice(low, low + step)
        found, norms = [], []
        for head in range(heads):
            at = head * HEAD_DIM
            query = qkv[here, at : at + HEAD_DIM]
            key = qkv[:, width + at : width + at + HEAD_DIM]
            value = qkv[:, 2 * width + at : 2 * width + at + HEAD_DIM]
            scores = dot(query, key, 1, 1) * 0.125 + mask[here, :]
            top = jnp.max(scores, axis=-1, keepdims=True)
            raised = jnp.exp(scores - top)
            total_raised = jnp.sum(raised, axis=-1, keepdims=True)
            probs = (raised * (1.0 / total_raised)).astype(LOW)
            found.append(dot(probs, value, 1, 0))
            norms.append(top + jnp.log(total_raised))
        mixed[here, :] = jnp.concatenate(found, axis=1).astype(LOW)
        for head in range(heads):
            lse[here, head : head + 1] = norms[head]


def feed_body(
    tok0, tok1, tok2, tok3, mixed0, mixed1, mixed2, mixed3, wo0, wo1, wo2, wo3, wf, rows, da,
    keep, send, middle, normed, active, grad_hidden,
):
    part = tok0.shape[0]
    half = 2 * part
    toks = (tok0, tok1, tok2, tok3)
    for number in range(2):
        here = slice(number * half, (number + 1) * half)
        source = jnp.concatenate([toks[2 * number][...], toks[2 * number + 1][...]], axis=0)
        total = source.astype(F32) + rows[0:1, :]
        for peer, (found, weight) in enumerate(((mixed0, wo0), (mixed1, wo1), (mixed2, wo2), (mixed3, wo3))):
            blocks = [found[(b ^ peer) * part : (b ^ peer) * part + part, :] for b in (2 * number, 2 * number + 1)]
            total += dot(jnp.concatenate(blocks, axis=0), weight[...], 1, 1)
        if number == 0:
            middle[...] = total
        scaled, _ = norm_parts(total)
        low_norm = (scaled * rows[4:5, :] + rows[5:6, :]).astype(LOW)
        normed[here, :] = low_norm
        hidden = dot(low_norm, wf[...], 1, 0) + rows[6:7, :]
        square = hidden * hidden
        bent = jnp.tanh(GELU_SCALE * hidden * (1.0 + 0.044715 * square))
        rise = 0.5 * (1.0 + bent)
        active[here, :] = (hidden * rise).astype(LOW)
        slope = rise + 0.5 * hidden * (1.0 - bent * bent) * (
            GELU_SCALE * (1.0 + 3 * 0.044715 * square)
        )
        grad_low = (da[here, :] * slope).astype(LOW)
        grad_hidden[here, :] = grad_low
        back = dot(grad_low, wf[...], 1, 1)
        if number == 0:
            keep[...] = back
        else:
            send[...] = back.astype(LOW)


def put_pieces(me, outs, parts):
    chunk = outs[0].shape[0]
    for step, out in enumerate(outs):
        place = pl.ds(row_start(me, step, chunk), chunk) if len(outs) > 1 else slice(None)
        low = 0
        for part in parts:
            high = low + part.shape[1]
            out[:, low:high] = part[place, :].astype(out.dtype)
            low = high


def piece_shapes(parts, width, cols):
    return [shape(width // parts, cols, LOW if step else F32) for step in range(parts)]


def feed_grad_body(scal, active, wp, normed, grad_hidden, cot, *refs):
    keep, send, fc_sum = refs[:3]
    pieces, whole = refs[3:-1], refs[-1]
    half = keep.shape[0]
    cols = wp.shape[1]
    whole[:, :cols] = dot(normed[...], grad_hidden[...], 0, 0)
    whole[:, cols:] = dot(cot[...], active[...], 0, 0)
    put_pieces(scal[0], pieces, [whole])
    keep[...] = dot(active[:half, :], wp[...], 1, 1)
    send[...] = dot(active[half:, :], wp[...], 1, 1).astype(LOW)
    fc_sum[...] = jnp.sum(grad_hidden[...].astype(F32), axis=0, keepdims=True)


def middle_body(part_two, far, middle, cot, rows, grad_low, grad_own, early):
    own = grad_own.shape[0]
    flipped = jnp.concatenate([far[own:, :], far[:own, :]], axis=0).astype(F32)
    grad = part_two[...] + flipped
    scaled, inverse = norm_parts(middle[...])
    cotangent = cot[: 2 * own, :].astype(F32)
    total = cotangent + norm_back(grad, scaled, inverse, rows[4:5, :])
    grad_low[...] = total.astype(LOW)
    grad_own[...] = total[:own]
    add = functools.partial(jnp.sum, axis=0, keepdims=True)
    empty = jnp.zeros((2, total.shape[1]), F32)
    early[...] = jnp.concatenate(
        [add(total[:own]), add(cotangent[:own]), empty, add(grad[:own] * scaled[:own]), add(grad[:own]), empty],
        axis=0,
    )


def attend_back_body(
    grad_half, grad_other, wo, wqkv, qkv, lse, tok0, tok1, tok2, tok3, early, doc_col, doc_row, pos_col, pos_row,
    keep, send, grad_qkv, late, qkv_sum, mask,
):
    total = qkv.shape[0]
    half = total // 2
    toks = (tok0, tok1, tok2, tok3)
    width = qkv.shape[1] // 3
    heads = width // HEAD_DIM
    fill_mask(mask, doc_col, doc_row, pos_col, pos_row)
    grad_attn = [dot(g[...], wo[...], 1, 0).astype(LOW) for g in (grad_half, grad_other)]
    query_grads = [[], []]
    key_grads, value_grads = [], []
    for head in range(heads):
        at = head * HEAD_DIM
        key = qkv[:, width + at : width + at + HEAD_DIM]
        value = qkv[:, 2 * width + at : 2 * width + at + HEAD_DIM]
        key_grad = value_grad = None
        for number in range(2):
            here = slice(number * half, (number + 1) * half)
            query = qkv[here, at : at + HEAD_DIM]
            grad = grad_attn[number][:, at : at + HEAD_DIM]
            scores = dot(query, key, 1, 1) * 0.125 + mask[here, :]
            probs = jnp.exp(scores - lse[here, head : head + 1])
            grad_probs = dot(grad, value, 1, 1)
            inner = jnp.sum(probs * grad_probs, axis=-1, keepdims=True)
            grad_scores = (probs * (grad_probs - inner)).astype(LOW)
            query_grads[number].append(dot(grad_scores, key, 1, 0) * 0.125)
            more_key = dot(grad_scores, query, 0, 0)
            more_value = dot(probs.astype(LOW), grad, 0, 0)
            key_grad = more_key if key_grad is None else key_grad + more_key
            value_grad = more_value if value_grad is None else value_grad + more_value
        key_grads.append(key_grad * 0.125)
        value_grads.append(value_grad)
    for number in range(2):
        here = slice(number * half, (number + 1) * half)
        grad_qkv[here, :] = jnp.concatenate(
            query_grads[number] + [k[here] for k in key_grads] + [v[here] for v in value_grads], axis=1
        ).astype(LOW)
    gain_sum = shift_sum = 0.0
    for number in range(2):
        here = slice(number * half, (number + 1) * half)
        back = dot(grad_qkv[here, :], wqkv[...], 1, 1)
        source = jnp.concatenate([toks[2 * number][...], toks[2 * number + 1][...]], axis=0)
        scaled, _ = norm_parts(source.astype(F32))
        gain_sum += jnp.sum(back * scaled, axis=0, keepdims=True)
        shift_sum += jnp.sum(back, axis=0, keepdims=True)
        if number == 0:
            keep[...] = back
        else:
            send[...] = back.astype(LOW)
    late[...] = jnp.concatenate([early[:2, :], gain_sum, shift_sum, early[4:, :]], axis=0)
    sums = jnp.sum(grad_qkv[...].astype(F32), axis=0, keepdims=True)
    qkv_sum[...] = jnp.concatenate([sums, jnp.zeros((7, sums.shape[1]), F32)], axis=0)


def last_grad_body(
    grad_half, grad_other, mixed, tok0, tok1, tok2, tok3, rows, grad_qkv, fc_sum, qkv_sum, sel, whole, lines, normed
):
    part = tok0.shape[0]
    half = 2 * part
    for number, source in enumerate((tok0, tok1, tok2, tok3)):
        scaled, _ = norm_parts(source[...].astype(F32))
        normed[number * part : (number + 1) * part, :] = (scaled * rows[2:3, :] + rows[3:4, :]).astype(LOW)
    split = grad_qkv.shape[1]
    whole[:, :split] = dot(normed[...], grad_qkv[...], 0, 0)
    whole[:, split:] = dot(grad_half[...], mixed[:half, :], 0, 0) + dot(grad_other[...], mixed[half:, :], 0, 0)
    count = qkv_sum.shape[1] // 3
    col = lax.broadcasted_iota(jnp.int32, qkv_sum.shape, 1)
    line = lax.broadcasted_iota(jnp.int32, qkv_sum.shape, 0)
    sums = qkv_sum[0:1, :]
    sums = jnp.where((line == 0) & (col < count) | (line == 1) & (col >= 2 * count), sums, 0.0)
    placed = lax.dot_general(
        sums, sel[...].astype(F32), (((1,), (1,)), ((), ())),
        preferred_element_type=F32, precision=lax.Precision.HIGHEST,
    )
    lines[...] = jnp.concatenate([fc_sum[...], placed[:7]], axis=0)


def last_cut_body(scal, whole, late, lines, *refs):
    pieces, cols = refs[:-1], refs[-1]
    line = jnp.concatenate([late[:6, :], lines[:3, :]], axis=0)
    lack = jnp.zeros((VEC_COLS - line.shape[0], line.shape[1]), F32)
    cols[...] = jnp.concatenate([line, lack], axis=0).T
    put_pieces(scal[0], pieces, [cols, whole])


def input_body(keep, far, middle_grad, own, rows, out):
    part = own.shape[0]
    grad = keep[:part, :] + far[...].astype(F32)
    scaled, inverse = norm_parts(own[...].astype(F32))
    out[...] = middle_grad[...] + norm_back(grad, scaled, inverse, rows[2:3, :])


def total_of(*refs):
    total = refs[0][...]
    for ref in refs[1:]:
        total = total + ref[...].astype(F32)
    return total


def sum_feed_body(*refs):
    total = total_of(*refs[:4])
    wfc, wproj = refs[4:]
    cols = wfc.shape[1]
    wfc[...] = total[:, :cols]
    wproj[...] = total[:, cols:]


def sum_last_body(*refs):
    total = total_of(*refs[:4])
    wqkv, wout, qv, *vecs = refs[4:]
    width = wout.shape[0]
    for number in range(3):
        low = VEC_COLS + number * width
        wqkv[number] = total[:, low : low + width]
    wout[...] = turned_wide(total[:, VEC_COLS + 3 * width :])
    turned_vecs = turned_wide(total[:, :VEC_COLS])
    for number, vec in enumerate(vecs):
        vec[...] = turned_vecs[number : number + 1]
    qv[...] = turned_vecs[7:9, : qv.shape[1]]


def local(
    tokens,
    segments,
    grad_out,
    w_qkv,
    b_qv,
    w_out,
    b_out,
    w_fc,
    b_fc,
    w_proj,
    b_proj,
    ln1_gain,
    ln1_bias,
    ln2_gain,
    ln2_bias,
):
    size = lax.axis_size("fsdp")
    direct = size == DIRECT_SIZE
    me = lax.axis_index("fsdp")
    chunk, hidden_cols = w_fc.shape
    own_rows, width = tokens.shape
    seq_rows = segments.shape[0]
    half = 2 * own_rows
    head_cols = w_out.shape[0]
    qkv_cols = 3 * head_cols
    qv_count = b_qv.shape[1]
    place = lax.axis_index("seq") * 2 + lax.axis_index("tensor")
    scal = jnp.stack([me, place]).astype(jnp.int32)
    parts = size if direct else 1

    near = swap(tokens, "tensor")
    toks = [tokens, near, swap(tokens, "seq"), swap(near, "seq")]

    vecs = [b_out, b_proj, ln1_gain, ln1_bias, ln2_gain, ln2_bias, b_fc]
    col = np.arange(qkv_cols)
    inner = col % head_cols
    source = (inner // qv_count) * chunk + inner % qv_count
    row_number = lax.broadcasted_iota(jnp.int32, (width, qkv_cols), 0)
    sel = (row_number == jnp.asarray(source, jnp.int32)[None, :]).astype(LOW)

    rows_shape = shape(8, width, F32)
    bias_shape = shape(8, qkv_cols, F32)
    if direct:
        first, second = on_core(
            pack_body,
            [shape(chunk, VEC_COLS + qkv_cols + head_cols, LOW), shape(chunk, 2 * hidden_cols, LOW)],
            [],
            [w_qkv, w_out, w_fc, w_proj.T, b_qv, *vecs],
            limit=62,
        )
        firsts = pieces_ring_first(first)
        seconds = pieces_mixed(second, [firsts[1], firsts[3]])
    else:
        lines = jnp.stack([*vecs, *jnp.pad(b_qv, ((0, 0), (0, chunk - qv_count)))])
        lack = jnp.zeros((chunk, VEC_COLS - lines.shape[0]), LOW)
        first = jnp.concatenate([lines.T, lack, w_qkv[0], w_qkv[1], w_qkv[2], w_out.T], axis=1)
        second = jnp.concatenate([w_fc, w_proj.T], axis=1)
        firsts = [lax.all_gather(first, "fsdp", axis=0, tiled=True)]
        seconds = [lax.all_gather(second, "fsdp", axis=0, tiled=True)]
        scal = scal * jnp.asarray([0, 1], jnp.int32)
    blocks = [place ^ b for b in range(4)]
    docs = jnp.concatenate([lax.dynamic_slice_in_dim(segments, b * own_rows, own_rows, 0) for b in blocks])
    spots = jnp.concatenate([b * own_rows + jnp.arange(own_rows, dtype=jnp.int32) for b in blocks])
    marks = [docs[:, None], docs[None, :], spots[:, None], spots[None, :]]

    mask_scratch = pltpu.VMEM((seq_rows, seq_rows), F32)
    normed_scratch = pltpu.VMEM((seq_rows, width), LOW)
    qkv, mixed, lse, wqkv, wo, rows = on_core(
        functools.partial(attend_body, parts),
        [
            shape(seq_rows, qkv_cols, LOW),
            shape(seq_rows, head_cols, LOW),
            shape(seq_rows, 128, F32),
            shape(width, qkv_cols, LOW),
            shape(width, head_cols, LOW),
            rows_shape,
        ],
        [scal],
        [*firsts, sel, *toks, *marks],
        [pltpu.VMEM((width, VEC_COLS), F32), normed_scratch, mask_scratch],
        flops=2 * seq_rows * (width * qkv_cols + 2 * head_cols * seq_rows),
    )
    wo_near = swap(after(wo, mixed), "tensor")
    wos = [wo, wo_near, swap(wo, "seq"), swap(wo_near, "seq")]
    mixed_near = swap(mixed, "tensor")
    mixeds = [mixed, mixed_near, swap(mixed, "seq"), swap(mixed_near, "seq")]

    square = 2 * seq_rows * width * hidden_cols
    wf, wp, da, cot = on_core(
        functools.partial(open_second_body, parts),
        [
            shape(width, hidden_cols, LOW),
            shape(width, hidden_cols, LOW),
            shape(seq_rows, hidden_cols, F32),
            shape(seq_rows, width, LOW),
        ],
        [scal],
        [*seconds, grad_out],
        flops=square,
    )
    keep, send, middle, normed_two, active, grad_hidden = on_core(
        feed_body,
        [
            shape(half, width, F32),
            shape(half, width, LOW),
            shape(half, width, F32),
            shape(seq_rows, width, LOW),
            shape(seq_rows, hidden_cols, LOW),
            shape(seq_rows, hidden_cols, LOW),
        ],
        [],
        [*toks, *mixeds, *wos, wf, rows, da],
        flops=3 * square,
    )
    part_two = keep + swap(send, "seq").astype(F32)
    far = swap(part_two.astype(LOW), "tensor")

    piece_cols = 2 * hidden_cols
    out_keep, out_send, fc_sum, *grad_ff = on_core(
        feed_grad_body,
        [shape(half, width, F32), shape(half, width, LOW), shape(1, hidden_cols, F32), *piece_shapes(parts, width, piece_cols)],
        [scal],
        [active, wp, normed_two, grad_hidden, after(cot, part_two)],
        [pltpu.VMEM((width, piece_cols), F32)],
        flops=3 * square,
    )
    out_half = out_keep + swap(out_send, "seq").astype(F32)
    out_far = swap(out_half[own_rows:].astype(LOW), "tensor")
    result = (middle[:own_rows] + out_half[:own_rows] + out_far.astype(F32) + rows[1:2]).astype(LOW)
    far = after(far, fc_sum)
    if direct:
        begun = sums_begin(grad_ff)
        far = after(far, begun[0], begun[2])
    grad_mid_half, grad_mid_own, early = on_core(
        middle_body,
        [shape(half, width, LOW), shape(own_rows, width, F32), rows_shape],
        [],
        [part_two, far, middle, cot, rows],
    )
    grad_mid_other = swap(grad_mid_half, "seq")

    if direct:
        got_ff = sums_end(grad_ff, begun)
    keep_one, send_one, grad_qkv, late, qkv_sum = on_core(
        attend_back_body,
        [
            shape(half, width, F32),
            shape(half, width, LOW),
            shape(seq_rows, qkv_cols, LOW),
            rows_shape,
            bias_shape,
        ],
        [],
        [grad_mid_half, grad_mid_other, wo, wqkv, qkv, lse, *toks, early, *marks],
        [mask_scratch],
        flops=2 * seq_rows * (width * (qkv_cols + head_cols) + 5 * head_cols * seq_rows),
    )
    part_one = keep_one + swap(send_one, "seq").astype(F32)
    far_one = swap(part_one[own_rows:].astype(LOW), "tensor")
    (grad_inputs,) = on_core(
        input_body,
        [shape(own_rows, width, F32)],
        [],
        [part_one, far_one, grad_mid_own, tokens, rows],
    )

    last_cols = VEC_COLS + qkv_cols + head_cols
    whole, lines = on_core(
        last_grad_body,
        [shape(width, qkv_cols + head_cols, F32), rows_shape],
        [],
        [grad_mid_half, grad_mid_other, mixed, *toks, rows, grad_qkv, fc_sum, qkv_sum, sel],
        [normed_scratch],
        flops=2 * seq_rows * width * (qkv_cols + head_cols),
    )
    late = late + swap(late, "tensor")
    late = after(late, part_one, lines)
    late = late + swap(late, "seq")
    if direct:
        late = after(late, *begun)
    grad_last = on_core(
        last_cut_body,
        piece_shapes(parts, width, last_cols),
        [scal],
        [whole, late, lines],
        [pltpu.VMEM((width, VEC_COLS), F32)],
    )

    if direct:
        begun = sums_begin(grad_last)
        begun[1] = after(begun[1], far_one, out_far)
        got_last = sums_end(grad_last, begun)
        grad_wfc, grad_wproj = on_core(
            sum_feed_body,
            [shape(chunk, hidden_cols, F32)] * 2,
            [],
            got_ff,
        )
        grad_wproj = grad_wproj.T
        grad_wqkv, grad_wout, grad_qv, *sums = on_core(
            sum_last_body,
            [jax.ShapeDtypeStruct((3, chunk, head_cols), F32), shape(head_cols, chunk, F32), shape(2, qv_count, F32)]
            + [shape(1, chunk, F32)] * 7,
            [],
            got_last,
        )
    else:
        sum_ff = lax.psum_scatter(grad_ff[0], "fsdp", scatter_dimension=0, tiled=True)
        sum_last = lax.psum_scatter(grad_last[0], "fsdp", scatter_dimension=0, tiled=True)
        grad_wfc, grad_wproj = sum_ff[:, :hidden_cols], sum_ff[:, hidden_cols:].T
        split = VEC_COLS + qkv_cols
        grad_wqkv = sum_last[:, VEC_COLS:split].reshape(chunk, 3, head_cols).transpose(1, 0, 2)
        grad_wout = sum_last[:, split:].T
        sums = sum_last[:, :7].T
        grad_qv = sum_last[:qv_count, 7:9].T

    return (
        result,
        grad_inputs,
        grad_wqkv,
        grad_wout,
        grad_wfc,
        grad_wproj,
        grad_qv,
        *[sums[number].reshape(chunk) for number in (0, 6, 1, 2, 3, 4, 5)],
    )


def solution(mesh):
    in_specs = (
        P(("fsdp", "seq", "tensor"), None),
        P("fsdp"),
        P("fsdp", None),
        P(None, "fsdp", ("seq", "tensor")),
        P(None, ("seq", "tensor", "fsdp")),
        P(("seq", "tensor"), "fsdp"),
        P("fsdp"),
        P("fsdp", ("seq", "tensor")),
        P(("seq", "tensor", "fsdp")),
        P(("seq", "tensor"), "fsdp"),
        P("fsdp"),
        P("fsdp"),
        P("fsdp"),
        P("fsdp"),
        P("fsdp"),
    )
    out_specs = (
        P(("fsdp", "seq", "tensor"), None),
        P(("fsdp", "seq", "tensor"), None),
        P(None, "fsdp", ("seq", "tensor")),
        P(("seq", "tensor"), "fsdp"),
        P("fsdp", ("seq", "tensor")),
        P(("seq", "tensor"), "fsdp"),
        P(None, ("seq", "tensor", "fsdp")),
        P("fsdp"),
        P(("seq", "tensor", "fsdp")),
        P("fsdp"),
        P("fsdp"),
        P("fsdp"),
        P("fsdp"),
        P("fsdp"),
    )
    return jax.shard_map(local, mesh=mesh, in_specs=in_specs, out_specs=out_specs, check_vma=False)
```

```python
import functools

import jax
import jax.numpy as jnp
import numpy as np
from jax import lax
from jax.experimental import pallas as pl
from jax.experimental.pallas import tpu as pltpu
from jax.sharding import PartitionSpec as P

HEAD_DIM = 64
DIRECT_SIZE = 8
STEPS = ((0, 0), (1, 0), (3, 1), (3, 0), (1, 1), (0, 1), (2, 0), (2, 1))
VEC_COLS = 128
LOW = jnp.bfloat16
F32 = jnp.float32
GELU_SCALE = float(np.sqrt(2.0 / np.pi))


def shape(rows, cols, dtype):
    return jax.ShapeDtypeStruct((rows, cols), dtype)


def on_core(body, outs, scalars, arrays, scratch=(), flops=0, limit=40, far=0):
    specs = [pl.BlockSpec(memory_space=pltpu.SMEM)] * len(scalars)
    specs += [pl.BlockSpec(memory_space=pltpu.HBM)] * far + [pl.BlockSpec()] * (len(arrays) - far)
    moved = sum(int(np.prod(a.shape)) * a.dtype.itemsize for a in arrays) + sum(
        int(np.prod(o.shape)) * o.dtype.itemsize for o in outs
    )
    return pl.pallas_call(
        body,
        out_shape=tuple(outs),
        in_specs=specs,
        out_specs=tuple(pl.BlockSpec() for _ in outs),
        scratch_shapes=list(scratch),
        compiler_params=pltpu.CompilerParams(vmem_limit_bytes=limit * 2**20),
        cost_estimate=pl.CostEstimate(flops=flops, bytes_accessed=moved, transcendentals=0),
    )(*scalars, *arrays)


def dot(left, right, left_dim, right_dim):
    return lax.dot_general(
        left, right, (((left_dim,), (right_dim,)), ((), ())), preferred_element_type=F32
    )


def norm_parts(values):
    center = values - jnp.mean(values, axis=-1, keepdims=True)
    spread = jnp.mean(center * center, axis=-1, keepdims=True)
    inverse = lax.rsqrt(spread + 1e-05)
    return center * inverse, inverse


def norm_back(cot, scaled, inverse, gain):
    inner = cot * gain
    first = jnp.mean(inner, axis=-1, keepdims=True)
    second = jnp.mean(inner * scaled, axis=-1, keepdims=True)
    return (inner - first - scaled * second) * inverse


def turned(value):
    count = value.shape[1]
    row = lax.broadcasted_iota(jnp.int32, (count, count), 0)
    col = lax.broadcasted_iota(jnp.int32, (count, count), 1)
    return dot((row == col).astype(F32).astype(LOW), value, 1, 1).astype(LOW)


def turned_wide(value):
    rows = value.shape[0]
    lack = -rows % 128
    if lack:
        value = jnp.concatenate([value, jnp.zeros((lack, value.shape[1]), value.dtype)], axis=0)
    return value.T[:, :rows]


def swap(value, axis):
    return lax.ppermute(value, axis, [(0, 1), (1, 0)])


def send(value, turn, flip):
    pairs = [(i, (i // 2 + turn) % 4 * 2 + (i % 2 ^ flip)) for i in range(DIRECT_SIZE)]
    return lax.ppermute(value, "fsdp", pairs)


def after(value, *earlier):
    return lax.optimization_barrier((value, *earlier))[0]


def pieces_ring_first(chunk):
    ahead, behind = send(chunk, 3, 0), send(chunk, 1, 0)
    other = send(chunk, 0, 1)
    far = send(ahead, 3, 0)
    across = [send(behind, 0, 1), send(ahead, 0, 1)]
    return [chunk, ahead, across[0], behind, across[1], other, far, send(far, 0, 1)]


def pieces_mixed(chunk, ring_free):
    ahead, behind = [send(after(chunk, *ring_free), turn, 0) for turn in (3, 1)]
    other = send(chunk, 0, 1)
    far = send(ahead, 3, 0)
    return [chunk, ahead, send(other, 1, 0), behind, send(ahead, 0, 1), other, far, send(far, 0, 1)]


def added(*values):
    total = values[0].astype(F32)
    for value in values[1:]:
        total = total + value.astype(F32)
    return total.astype(LOW)


def sums_begin(pieces):
    return [send(pieces[7], 0, 1), send(pieces[4], 0, 1), send(pieces[2], 3, 0), send(pieces[3], 3, 0)]


def sums_end(pieces, got):
    far = send(added(after(pieces[6], got[2]), got[0]), 1, 0)
    other = send(added(after(pieces[5], far), got[2]), 0, 1)
    ahead = send(added(pieces[1], got[1], far), 1, 0)
    return [pieces[0], got[3], other, ahead]


def row_start(me, step, rows):
    turn, flip = STEPS[step]
    pair = lax.rem(lax.div(me, 2) + turn, 4)
    return pl.multiple_of((pair * 2 + (lax.rem(me, 2) ^ flip)) * rows, rows)


def pack_body(wqkv, wout, wfc, wproj, bqv, *refs):
    vecs, first, second = refs[:-2], refs[-2], refs[-1]
    rows = wqkv.shape[1]
    lines = [vec[...].astype(F32).reshape(1, rows) for vec in vecs]
    lack = jnp.zeros((2, rows - bqv.shape[1]), F32)
    lines.append(jnp.concatenate([bqv[...].astype(F32), lack], axis=1))
    lines.append(jnp.zeros((VEC_COLS - len(vecs) - 2, rows), F32))
    cols = jnp.concatenate(lines, axis=0)
    lack = -rows % 128
    if lack:
        cols = jnp.concatenate([cols, jnp.zeros((VEC_COLS, lack), F32)], axis=1)
    cols = cols.T[:rows].astype(LOW)
    first[...] = jnp.concatenate([cols, wqkv[0], wqkv[1], wqkv[2], turned(wout[...])], axis=1)
    second[...] = jnp.concatenate([wfc[...], wproj[...]], axis=1)


def open_second_body(size, *refs):
    pieces, (grad, wf, wp, da, cot) = refs[:size], refs[size:]
    chunk = pieces[-1].shape[0]
    cols = wf.shape[1]
    own = cot.shape[0] // 4
    for step, piece in enumerate(pieces):
        place = pl.ds(row_start(lax.axis_index("fsdp"), step, chunk) if size > 1 else 0, chunk)
        wf[place, :] = piece[:, :cols]
        wp[place, :] = piece[:, cols:]
    for block in range(4):
        start = pl.multiple_of((core_place() ^ block) * own, own)
        cot[block * own : (block + 1) * own, :] = grad[pl.ds(start, own), :]
    da[...] = dot(cot[...], wp[...], 1, 0)


def prepare_body(tok0, tok1, tok2, tok3, doc_col, doc_row, pos_col, pos_row, scaled, mask):
    part = tok0.shape[0]
    for number, source in enumerate((tok0, tok1, tok2, tok3)):
        here = slice(number * part, (number + 1) * part)
        scaled[here, :] = norm_parts(source[...].astype(F32))[0]
        seen = (doc_col[here, :] == doc_row[...]) & (pos_row[...] <= pos_col[here, :])
        mask[here, :] = jnp.where(seen, 0.0, -1e30)


def core_place():
    return lax.axis_index("seq") * 2 + lax.axis_index("tensor")


def halves(place, rows):
    half = rows // 2
    first = pl.multiple_of(lax.div(place, 2) * half, half)
    return pl.ds(first, half), pl.ds(pl.multiple_of(half - first, half), half)


def softmax(scores):
    top = jnp.max(scores, axis=-1, keepdims=True)
    raised = jnp.exp(scores - top)
    total = jnp.sum(raised, axis=-1, keepdims=True)
    return (raised * (1.0 / total)).astype(LOW), top + jnp.log(total)


def attend_body(size, *refs):
    pieces, refs = refs[:size], refs[size:]
    sel, scaled, mask = refs[:3]
    qkv, mixed, lse, wqkv, wo, rows, opened, normed, arrived = refs[3:]
    chunk = pieces[0].shape[0]
    split = VEC_COLS + wqkv.shape[1]
    end = split + wo.shape[1]
    copies = []
    for step, piece in enumerate(pieces):
        place = pl.ds(row_start(lax.axis_index("fsdp"), step, chunk) if size > 1 else 0, chunk)
        copies.append(pltpu.make_async_copy(piece, opened.at[place, :], arrived.at[step]))
        copies[-1].start()
    for copy in copies:
        copy.wait()
    wqkv[...] = opened[:, VEC_COLS:split]
    wo[...] = opened[:, split:end]
    wide = opened[:, :VEC_COLS].astype(F32).T
    rows[...] = wide[:8]
    spread = dot(wide[:16].astype(LOW), sel[...], 1, 0)
    col = lax.broadcasted_iota(jnp.int32, (1, qkv.shape[1]), 1)
    count = wo.shape[1]
    bias = jnp.where(col < count, spread[7:8], jnp.where(col >= 2 * count, spread[8:9], 0.0))
    total = qkv.shape[0]
    normed[...] = (scaled[...] * wide[2:3] + wide[3:4]).astype(LOW)
    qkv[...] = (dot(normed[...], wqkv[...], 1, 0) + bias).astype(LOW)
    width = qkv.shape[1] // 3
    heads = width // HEAD_DIM
    half = total // 2
    found_low, found_high = [], []
    low, high = halves(core_place(), total)
    for head in range(heads):
        at = head * HEAD_DIM
        query_low, key_low, value_low = [qkv[low, n * width + at : n * width + at + HEAD_DIM] for n in range(3)]
        query_high, key_high, value_high = [qkv[high, n * width + at : n * width + at + HEAD_DIM] for n in range(3)]
        probs, norm = softmax(dot(query_low, key_low, 1, 1) * 0.125 + mask[:half, :half])
        lse[:half, head : head + 1] = norm
        found_low.append(dot(probs, value_low, 1, 0))
        scores = jnp.concatenate([dot(query_high, key_low, 1, 1), dot(query_high, key_high, 1, 1)], axis=1)
        probs, norm = softmax(scores * 0.125 + mask[half:, :])
        lse[half:, head : head + 1] = norm
        found_high.append(dot(probs[:, :half], value_low, 1, 0) + dot(probs[:, half:], value_high, 1, 0))
    mixed[low, :] = jnp.concatenate(found_low, axis=1).astype(LOW)
    mixed[high, :] = jnp.concatenate(found_high, axis=1).astype(LOW)


def feed_body(
    tok0, tok1, tok2, tok3, mixed0, mixed1, mixed2, mixed3, wo0, wo1, wo2, wo3, wf, rows, da,
    keep, send, middle, normed, active, grad_hidden,
):
    part = tok0.shape[0]
    half = 2 * part
    toks = (tok0, tok1, tok2, tok3)
    for number in range(2):
        here = slice(number * half, (number + 1) * half)
        source = jnp.concatenate([toks[2 * number][...], toks[2 * number + 1][...]], axis=0)
        total = source.astype(F32) + rows[0:1, :]
        for peer, (found, weight) in enumerate(((mixed0, wo0), (mixed1, wo1), (mixed2, wo2), (mixed3, wo3))):
            blocks = [found[(b ^ peer) * part : (b ^ peer) * part + part, :] for b in (2 * number, 2 * number + 1)]
            total += dot(jnp.concatenate(blocks, axis=0), weight[...], 1, 1)
        if number == 0:
            middle[...] = total
        scaled, _ = norm_parts(total)
        low_norm = (scaled * rows[4:5, :] + rows[5:6, :]).astype(LOW)
        normed[here, :] = low_norm
        hidden = dot(low_norm, wf[...], 1, 0) + rows[6:7, :]
        square = hidden * hidden
        bent = jnp.tanh(GELU_SCALE * hidden * (1.0 + 0.044715 * square))
        rise = 0.5 * (1.0 + bent)
        active[here, :] = (hidden * rise).astype(LOW)
        slope = rise + 0.5 * hidden * (1.0 - bent * bent) * (
            GELU_SCALE * (1.0 + 3 * 0.044715 * square)
        )
        grad_low = (da[here, :] * slope).astype(LOW)
        grad_hidden[here, :] = grad_low
        back = dot(grad_low, wf[...], 1, 1)
        if number == 0:
            keep[...] = back
        else:
            send[...] = back.astype(LOW)


def put_pieces(me, outs, parts):
    chunk = outs[0].shape[0]
    for step, out in enumerate(outs):
        place = pl.ds(row_start(me, step, chunk), chunk) if len(outs) > 1 else slice(None)
        low = 0
        for part in parts:
            high = low + part.shape[1]
            out[:, low:high] = part[place, :].astype(out.dtype)
            low = high


def piece_shapes(parts, width, cols):
    return [shape(width // parts, cols, LOW if step else F32) for step in range(parts)]


def feed_grad_body(active, wp, normed, grad_hidden, cot, *refs):
    keep, send, fc_sum = refs[:3]
    pieces, whole = refs[3:-1], refs[-1]
    half = keep.shape[0]
    cols = wp.shape[1]
    whole[:, :cols] = dot(normed[...], grad_hidden[...], 0, 0)
    whole[:, cols:] = dot(cot[...], active[...], 0, 0)
    put_pieces(lax.axis_index("fsdp"), pieces, [whole])
    keep[...] = dot(active[:half, :], wp[...], 1, 1)
    send[...] = dot(active[half:, :], wp[...], 1, 1).astype(LOW)
    fc_sum[...] = jnp.sum(grad_hidden[...].astype(F32), axis=0, keepdims=True)


def middle_body(part_two, far, middle, cot, rows, grad_low, grad_own, early):
    own = grad_own.shape[0]
    flipped = jnp.concatenate([far[own:, :], far[:own, :]], axis=0).astype(F32)
    grad = part_two[...] + flipped
    scaled, inverse = norm_parts(middle[...])
    cotangent = cot[: 2 * own, :].astype(F32)
    total = cotangent + norm_back(grad, scaled, inverse, rows[4:5, :])
    grad_low[...] = total.astype(LOW)
    grad_own[...] = total[:own]
    add = functools.partial(jnp.sum, axis=0, keepdims=True)
    empty = jnp.zeros((2, total.shape[1]), F32)
    early[...] = jnp.concatenate(
        [add(total[:own]), add(cotangent[:own]), empty, add(grad[:own] * scaled[:own]), add(grad[:own]), empty],
        axis=0,
    )


def attend_back_body(
    grad_half, grad_other, wo, wqkv, qkv, lse, scaled, mask, early,
    keep, send, grad_qkv, late, qkv_sum, grad_attn,
):
    total = qkv.shape[0]
    half = total // 2
    width = qkv.shape[1] // 3
    heads = width // HEAD_DIM
    grad_attn[:half, :] = dot(grad_half[...], wo[...], 1, 0).astype(LOW)
    grad_attn[half:, :] = dot(grad_other[...], wo[...], 1, 0).astype(LOW)
    low, high = halves(core_place(), total)
    found_low, found_high = [[], [], []], [[], [], []]
    for head in range(heads):
        at = head * HEAD_DIM
        query_low, key_low, value_low = [qkv[low, n * width + at : n * width + at + HEAD_DIM] for n in range(3)]
        query_high, key_high, value_high = [qkv[high, n * width + at : n * width + at + HEAD_DIM] for n in range(3)]
        grad_low, grad_high = grad_attn[low, at : at + HEAD_DIM], grad_attn[high, at : at + HEAD_DIM]
        scores = dot(query_low, key_low, 1, 1) * 0.125 + mask[:half, :half]
        probs = jnp.exp(scores - lse[:half, head : head + 1])
        grad_probs = dot(grad_low, value_low, 1, 1)
        inner = jnp.sum(probs * grad_probs, axis=-1, keepdims=True)
        first = (probs * (grad_probs - inner)).astype(LOW)
        first_probs = probs.astype(LOW)
        scores = jnp.concatenate([dot(query_high, key_low, 1, 1), dot(query_high, key_high, 1, 1)], axis=1)
        probs = jnp.exp(scores * 0.125 + mask[half:, :] - lse[half:, head : head + 1])
        grad_probs = jnp.concatenate([dot(grad_high, value_low, 1, 1), dot(grad_high, value_high, 1, 1)], axis=1)
        inner = jnp.sum(probs * grad_probs, axis=-1, keepdims=True)
        second = (probs * (grad_probs - inner)).astype(LOW)
        second_probs = probs.astype(LOW)
        found_low[0].append(dot(first, key_low, 1, 0) * 0.125)
        found_high[0].append((dot(second[:, :half], key_low, 1, 0) + dot(second[:, half:], key_high, 1, 0)) * 0.125)
        found_low[1].append((dot(first, query_low, 0, 0) + dot(second[:, :half], query_high, 0, 0)) * 0.125)
        found_high[1].append(dot(second[:, half:], query_high, 0, 0) * 0.125)
        found_low[2].append(dot(first_probs, grad_low, 0, 0) + dot(second_probs[:, :half], grad_high, 0, 0))
        found_high[2].append(dot(second_probs[:, half:], grad_high, 0, 0))
    grad_qkv[low, :] = jnp.concatenate(sum(found_low, []), axis=1).astype(LOW)
    grad_qkv[high, :] = jnp.concatenate(sum(found_high, []), axis=1).astype(LOW)
    gain_sum = shift_sum = 0.0
    for number in range(2):
        here = slice(number * half, (number + 1) * half)
        back = dot(grad_qkv[here, :], wqkv[...], 1, 1)
        gain_sum += jnp.sum(back * scaled[here, :], axis=0, keepdims=True)
        shift_sum += jnp.sum(back, axis=0, keepdims=True)
        if number == 0:
            keep[...] = back
        else:
            send[...] = back.astype(LOW)
    late[...] = jnp.concatenate([early[:2, :], gain_sum, shift_sum, early[4:, :]], axis=0)
    sums = jnp.sum(grad_qkv[...].astype(F32), axis=0, keepdims=True)
    qkv_sum[...] = jnp.concatenate([sums, jnp.zeros((7, sums.shape[1]), F32)], axis=0)


def last_grad_body(
    grad_half, grad_other, mixed, scaled, rows, grad_qkv, fc_sum, qkv_sum, sel, whole, lines, normed
):
    half = grad_half.shape[0]
    normed[...] = (scaled[...] * rows[2:3, :] + rows[3:4, :]).astype(LOW)
    split = grad_qkv.shape[1]
    whole[:, :split] = dot(normed[...], grad_qkv[...], 0, 0)
    whole[:, split:] = dot(grad_half[...], mixed[:half, :], 0, 0) + dot(grad_other[...], mixed[half:, :], 0, 0)
    count = qkv_sum.shape[1] // 3
    col = lax.broadcasted_iota(jnp.int32, qkv_sum.shape, 1)
    line = lax.broadcasted_iota(jnp.int32, qkv_sum.shape, 0)
    sums = qkv_sum[0:1, :]
    sums = jnp.where((line == 0) & (col < count) | (line == 1) & (col >= 2 * count), sums, 0.0)
    placed = lax.dot_general(
        sums, sel[...].astype(F32), (((1,), (1,)), ((), ())),
        preferred_element_type=F32, precision=lax.Precision.HIGHEST,
    )
    lines[...] = jnp.concatenate([fc_sum[...], placed[:7]], axis=0)


def last_cut_body(whole, late, lines, *refs):
    pieces, cols = refs[:-1], refs[-1]
    line = jnp.concatenate([late[:6, :], lines[:3, :]], axis=0)
    lack = jnp.zeros((VEC_COLS - line.shape[0], line.shape[1]), F32)
    cols[...] = jnp.concatenate([line, lack], axis=0).T
    put_pieces(lax.axis_index("fsdp"), pieces, [cols, whole])


def input_body(keep, far, middle_grad, own, rows, out):
    part = own.shape[0]
    grad = keep[:part, :] + far[...].astype(F32)
    scaled, inverse = norm_parts(own[...].astype(F32))
    out[...] = middle_grad[...] + norm_back(grad, scaled, inverse, rows[2:3, :])


def total_of(*refs):
    total = refs[0][...]
    for ref in refs[1:]:
        total = total + ref[...].astype(F32)
    return total


def sum_feed_body(*refs):
    total = total_of(*refs[:4])
    wfc, wproj = refs[4:]
    cols = wfc.shape[1]
    wfc[...] = total[:, :cols]
    wproj[...] = total[:, cols:]


def sum_last_body(*refs):
    total = total_of(*refs[:4])
    wqkv, wout, qv, *vecs = refs[4:]
    width = wout.shape[0]
    for number in range(3):
        low = VEC_COLS + number * width
        wqkv[number] = total[:, low : low + width]
    wout[...] = turned_wide(total[:, VEC_COLS + 3 * width :])
    turned_vecs = turned_wide(total[:, :VEC_COLS])
    for number, vec in enumerate(vecs):
        vec[...] = turned_vecs[number : number + 1]
    qv[...] = turned_vecs[7:9, : qv.shape[1]]


def local(
    tokens,
    segments,
    grad_out,
    w_qkv,
    b_qv,
    w_out,
    b_out,
    w_fc,
    b_fc,
    w_proj,
    b_proj,
    ln1_gain,
    ln1_bias,
    ln2_gain,
    ln2_bias,
):
    size = lax.axis_size("fsdp")
    direct = size == DIRECT_SIZE
    chunk, hidden_cols = w_fc.shape
    own_rows, width = tokens.shape
    seq_rows = segments.shape[0]
    half = 2 * own_rows
    head_cols = w_out.shape[0]
    qkv_cols = 3 * head_cols
    qv_count = b_qv.shape[1]
    parts = size if direct else 1

    near = swap(tokens, "tensor")
    toks = [tokens, near, swap(tokens, "seq"), swap(near, "seq")]

    vecs = [b_out, b_proj, ln1_gain, ln1_bias, ln2_gain, ln2_bias, b_fc]
    col = np.arange(qkv_cols)
    inner = col % head_cols
    source = (inner // qv_count) * chunk + inner % qv_count
    row_number = lax.broadcasted_iota(jnp.int32, (width, qkv_cols), 0)
    sel = (row_number == jnp.asarray(source, jnp.int32)[None, :]).astype(LOW)

    blocks = [lax.axis_index("tensor") ^ b for b in range(4)]
    docs = jnp.concatenate([lax.dynamic_slice_in_dim(segments, b * own_rows, own_rows, 0) for b in blocks])
    spots = jnp.concatenate([b * own_rows + jnp.arange(own_rows, dtype=jnp.int32) for b in blocks])
    marks = [docs[:, None], docs[None, :], spots[:, None], spots[None, :]]
    scaled_one, mask = on_core(
        prepare_body,
        [shape(seq_rows, width, F32), shape(seq_rows, seq_rows, F32)],
        [],
        [*toks, *marks],
    )
    rows_shape = shape(8, width, F32)
    bias_shape = shape(8, qkv_cols, F32)
    if direct:
        first, second = on_core(
            pack_body,
            [shape(chunk, VEC_COLS + qkv_cols + head_cols, LOW), shape(chunk, 2 * hidden_cols, LOW)],
            [],
            [w_qkv, w_out, w_fc, w_proj.T, b_qv, *vecs],
            limit=62,
        )
        firsts = pieces_ring_first(first)
        seconds = pieces_mixed(second, [firsts[1], firsts[3]])
    else:
        lines = jnp.stack([*vecs, *jnp.pad(b_qv, ((0, 0), (0, chunk - qv_count)))])
        lack = jnp.zeros((chunk, VEC_COLS - lines.shape[0]), LOW)
        first = jnp.concatenate([lines.T, lack, w_qkv[0], w_qkv[1], w_qkv[2], w_out.T], axis=1)
        second = jnp.concatenate([w_fc, w_proj.T], axis=1)
        firsts = [lax.all_gather(first, "fsdp", axis=0, tiled=True)]
        seconds = [lax.all_gather(second, "fsdp", axis=0, tiled=True)]
    normed_scratch = pltpu.VMEM((seq_rows, width), LOW)
    qkv, mixed, lse, wqkv, wo, rows = on_core(
        functools.partial(attend_body, parts),
        [
            shape(seq_rows, qkv_cols, LOW),
            shape(seq_rows, head_cols, LOW),
            shape(seq_rows, 128, F32),
            shape(width, qkv_cols, LOW),
            shape(width, head_cols, LOW),
            rows_shape,
        ],
        [],
        [*firsts, sel, scaled_one, mask],
        [
            pltpu.VMEM((width, VEC_COLS + qkv_cols + head_cols), LOW),
            normed_scratch,
            pltpu.SemaphoreType.DMA((parts,)),
        ],
        far=parts,
        flops=2 * seq_rows * (width * qkv_cols + 2 * head_cols * seq_rows),
    )
    wo_near = swap(after(wo, mixed), "tensor")
    wos = [wo, wo_near, swap(wo, "seq"), swap(wo_near, "seq")]
    mixed_near = swap(mixed, "tensor")
    mixeds = [mixed, mixed_near, swap(mixed, "seq"), swap(mixed_near, "seq")]

    square = 2 * seq_rows * width * hidden_cols
    wf, wp, da, cot = on_core(
        functools.partial(open_second_body, parts),
        [
            shape(width, hidden_cols, LOW),
            shape(width, hidden_cols, LOW),
            shape(seq_rows, hidden_cols, F32),
            shape(seq_rows, width, LOW),
        ],
        [],
        [*seconds, grad_out],
        flops=square,
    )
    keep, send, middle, normed_two, active, grad_hidden = on_core(
        feed_body,
        [
            shape(half, width, F32),
            shape(half, width, LOW),
            shape(half, width, F32),
            shape(seq_rows, width, LOW),
            shape(seq_rows, hidden_cols, LOW),
            shape(seq_rows, hidden_cols, LOW),
        ],
        [],
        [*toks, *mixeds, *wos, wf, rows, da],
        flops=3 * square,
    )
    from_core = swap(send, "seq")

    piece_cols = 2 * hidden_cols
    out_keep, out_send, fc_sum, *grad_ff = on_core(
        feed_grad_body,
        [shape(half, width, F32), shape(half, width, LOW), shape(1, hidden_cols, F32), *piece_shapes(parts, width, piece_cols)],
        [],
        [active, wp, normed_two, grad_hidden, cot],
        [pltpu.VMEM((width, piece_cols), F32)],
        flops=3 * square,
    )
    out_half = out_keep + swap(out_send, "seq").astype(F32)
    out_far = swap(out_half[own_rows:].astype(LOW), "tensor")
    result = (middle[:own_rows] + out_half[:own_rows] + out_far.astype(F32) + rows[1:2]).astype(LOW)
    part_two = keep + after(from_core, fc_sum).astype(F32)
    far = swap(part_two.astype(LOW), "tensor")
    if direct:
        begun = sums_begin(grad_ff)
        far = after(far, begun[0], begun[2])
    grad_mid_half, grad_mid_own, early = on_core(
        middle_body,
        [shape(half, width, LOW), shape(own_rows, width, F32), rows_shape],
        [],
        [part_two, far, middle, cot, rows],
    )
    grad_mid_other = swap(grad_mid_half, "seq")

    if direct:
        got_ff = sums_end(grad_ff, begun)
    keep_one, send_one, grad_qkv, late, qkv_sum = on_core(
        attend_back_body,
        [
            shape(half, width, F32),
            shape(half, width, LOW),
            shape(seq_rows, qkv_cols, LOW),
            rows_shape,
            bias_shape,
        ],
        [],
        [grad_mid_half, grad_mid_other, wo, wqkv, qkv, lse, scaled_one, mask, early],
        [pltpu.VMEM((seq_rows, head_cols), LOW)],
        flops=2 * seq_rows * (width * (qkv_cols + head_cols) + 5 * head_cols * seq_rows),
    )
    part_one = keep_one + swap(send_one, "seq").astype(F32)
    far_one = swap(part_one[own_rows:].astype(LOW), "tensor")
    (grad_inputs,) = on_core(
        input_body,
        [shape(own_rows, width, F32)],
        [],
        [part_one, far_one, grad_mid_own, tokens, rows],
    )

    last_cols = VEC_COLS + qkv_cols + head_cols
    whole, lines = on_core(
        last_grad_body,
        [shape(width, qkv_cols + head_cols, F32), rows_shape],
        [],
        [grad_mid_half, grad_mid_other, mixed, scaled_one, rows, grad_qkv, fc_sum, qkv_sum, sel],
        [normed_scratch],
        flops=2 * seq_rows * width * (qkv_cols + head_cols),
    )
    late = late + swap(late, "tensor")
    late = after(late, part_one, lines)
    late = late + swap(late, "seq")
    if direct:
        late = after(late, *begun)
    grad_last = on_core(
        last_cut_body,
        piece_shapes(parts, width, last_cols),
        [],
        [whole, late, lines],
        [pltpu.VMEM((width, VEC_COLS), F32)],
    )

    if direct:
        begun = sums_begin(grad_last)
        begun[1] = after(begun[1], far_one, out_far)
        got_last = sums_end(grad_last, begun)
        grad_wfc, grad_wproj = on_core(
            sum_feed_body,
            [shape(chunk, hidden_cols, F32)] * 2,
            [],
            got_ff,
        )
        grad_wproj = grad_wproj.T
        grad_wqkv, grad_wout, grad_qv, *sums = on_core(
            sum_last_body,
            [jax.ShapeDtypeStruct((3, chunk, head_cols), F32), shape(head_cols, chunk, F32), shape(2, qv_count, F32)]
            + [shape(1, chunk, F32)] * 7,
            [],
            got_last,
        )
    else:
        sum_ff = lax.psum_scatter(grad_ff[0], "fsdp", scatter_dimension=0, tiled=True)
        sum_last = lax.psum_scatter(grad_last[0], "fsdp", scatter_dimension=0, tiled=True)
        grad_wfc, grad_wproj = sum_ff[:, :hidden_cols], sum_ff[:, hidden_cols:].T
        split = VEC_COLS + qkv_cols
        grad_wqkv = sum_last[:, VEC_COLS:split].reshape(chunk, 3, head_cols).transpose(1, 0, 2)
        grad_wout = sum_last[:, split:].T
        sums = sum_last[:, :7].T
        grad_qv = sum_last[:qv_count, 7:9].T

    return (
        result,
        grad_inputs,
        grad_wqkv,
        grad_wout,
        grad_wfc,
        grad_wproj,
        grad_qv,
        *[sums[number].reshape(chunk) for number in (0, 6, 1, 2, 3, 4, 5)],
    )


def solution(mesh):
    in_specs = (
        P(("fsdp", "seq", "tensor"), None),
        P("fsdp"),
        P("fsdp", None),
        P(None, "fsdp", ("seq", "tensor")),
        P(None, ("seq", "tensor", "fsdp")),
        P(("seq", "tensor"), "fsdp"),
        P("fsdp"),
        P("fsdp", ("seq", "tensor")),
        P(("seq", "tensor", "fsdp")),
        P(("seq", "tensor"), "fsdp"),
        P("fsdp"),
        P("fsdp"),
        P("fsdp"),
        P("fsdp"),
        P("fsdp"),
    )
    out_specs = (
        P(("fsdp", "seq", "tensor"), None),
        P(("fsdp", "seq", "tensor"), None),
        P(None, "fsdp", ("seq", "tensor")),
        P(("seq", "tensor"), "fsdp"),
        P("fsdp", ("seq", "tensor")),
        P(("seq", "tensor"), "fsdp"),
        P(None, ("seq", "tensor", "fsdp")),
        P("fsdp"),
        P(("seq", "tensor", "fsdp")),
        P("fsdp"),
        P("fsdp"),
        P("fsdp"),
        P("fsdp"),
        P("fsdp"),
    )
    return jax.shard_map(local, mesh=mesh, in_specs=in_specs, out_specs=out_specs, check_vma=False)
```

```python
import functools

import jax
import jax.numpy as jnp
import numpy as np
from jax import lax
from jax.experimental import pallas as pl
from jax.experimental.pallas import tpu as pltpu
from jax.sharding import PartitionSpec as P

HEAD_DIM = 64
DIRECT_SIZE = 8
STEPS = ((0, 0), (1, 0), (3, 1), (3, 0), (1, 1), (0, 1), (2, 0), (2, 1))
VEC_COLS = 128
LOW = jnp.bfloat16
F32 = jnp.float32
GELU_SCALE = float(np.sqrt(2.0 / np.pi))


def shape(rows, cols, dtype):
    return jax.ShapeDtypeStruct((rows, cols), dtype)


def on_core(body, outs, scalars, arrays, scratch=(), flops=0, limit=40, far=0):
    specs = [pl.BlockSpec(memory_space=pltpu.SMEM)] * len(scalars)
    specs += [pl.BlockSpec(memory_space=pltpu.HBM)] * far + [pl.BlockSpec()] * (len(arrays) - far)
    moved = sum(int(np.prod(a.shape)) * a.dtype.itemsize for a in arrays) + sum(
        int(np.prod(o.shape)) * o.dtype.itemsize for o in outs
    )
    return pl.pallas_call(
        body,
        out_shape=tuple(outs),
        in_specs=specs,
        out_specs=tuple(pl.BlockSpec() for _ in outs),
        scratch_shapes=list(scratch),
        compiler_params=pltpu.CompilerParams(vmem_limit_bytes=limit * 2**20),
        cost_estimate=pl.CostEstimate(flops=flops, bytes_accessed=moved, transcendentals=0),
    )(*scalars, *arrays)


def dot(left, right, left_dim, right_dim):
    return lax.dot_general(
        left, right, (((left_dim,), (right_dim,)), ((), ())), preferred_element_type=F32
    )


def norm_parts(values):
    center = values - jnp.mean(values, axis=-1, keepdims=True)
    spread = jnp.mean(center * center, axis=-1, keepdims=True)
    inverse = lax.rsqrt(spread + 1e-05)
    return center * inverse, inverse


def norm_back(cot, scaled, inverse, gain):
    inner = cot * gain
    first = jnp.mean(inner, axis=-1, keepdims=True)
    second = jnp.mean(inner * scaled, axis=-1, keepdims=True)
    return (inner - first - scaled * second) * inverse


def turned(value):
    count = value.shape[1]
    row = lax.broadcasted_iota(jnp.int32, (count, count), 0)
    col = lax.broadcasted_iota(jnp.int32, (count, count), 1)
    return dot((row == col).astype(F32).astype(LOW), value, 1, 1).astype(LOW)


def turned_wide(value):
    rows = value.shape[0]
    lack = -rows % 128
    if lack:
        value = jnp.concatenate([value, jnp.zeros((lack, value.shape[1]), value.dtype)], axis=0)
    return value.T[:, :rows]


def swap(value, axis):
    return lax.ppermute(value, axis, [(0, 1), (1, 0)])


def send(value, turn, flip):
    pairs = [(i, (i // 2 + turn) % 4 * 2 + (i % 2 ^ flip)) for i in range(DIRECT_SIZE)]
    return lax.ppermute(value, "fsdp", pairs)


def after(value, *earlier):
    return lax.optimization_barrier((value, *earlier))[0]


def pieces_ring_first(chunk):
    ahead, behind = send(chunk, 3, 0), send(chunk, 1, 0)
    other = send(chunk, 0, 1)
    far = send(ahead, 3, 0)
    across = [send(behind, 0, 1), send(ahead, 0, 1)]
    return [chunk, ahead, across[0], behind, across[1], other, far, send(far, 0, 1)]


def pieces_mixed(chunk, ring_free, ready):
    ahead, behind = [send(after(chunk, *ring_free), turn, 0) for turn in (3, 1)]
    other = send(chunk, 0, 1)
    far = send(after(ahead, ready), 3, 0)
    return [chunk, ahead, send(other, 1, 0), behind, send(ahead, 0, 1), other, far, send(far, 0, 1)]


def added(*values):
    total = values[0].astype(F32)
    for value in values[1:]:
        total = total + value.astype(F32)
    return total.astype(LOW)


def sums_begin(pieces):
    return [send(pieces[7], 0, 1), send(pieces[4], 0, 1), send(pieces[2], 3, 0), send(pieces[3], 3, 0)]


def sums_end(pieces, got):
    far = send(added(after(pieces[6], got[2]), got[0]), 1, 0)
    other = send(added(after(pieces[5], far), got[2]), 0, 1)
    ahead = send(added(pieces[1], got[1], far), 1, 0)
    return [pieces[0], got[3], other, ahead]


def row_start(me, step, rows):
    turn, flip = STEPS[step]
    pair = lax.rem(lax.div(me, 2) + turn, 4)
    return pl.multiple_of((pair * 2 + (lax.rem(me, 2) ^ flip)) * rows, rows)


def pack_body(wqkv, wout, bqv, *refs):
    vecs, first = refs[:-1], refs[-1]
    rows = wqkv.shape[1]
    lines = [vec[...].astype(F32).reshape(1, rows) for vec in vecs]
    lack = jnp.zeros((2, rows - bqv.shape[1]), F32)
    lines.append(jnp.concatenate([bqv[...].astype(F32), lack], axis=1))
    lines.append(jnp.zeros((VEC_COLS - len(vecs) - 2, rows), F32))
    cols = jnp.concatenate(lines, axis=0)
    lack = -rows % 128
    if lack:
        cols = jnp.concatenate([cols, jnp.zeros((VEC_COLS, lack), F32)], axis=1)
    cols = cols.T[:rows].astype(LOW)
    first[...] = jnp.concatenate([cols, wqkv[0], wqkv[1], wqkv[2], turned(wout[...])], axis=1)


def pack_second_body(wfc, wproj, second):
    second[:, : wfc.shape[1]] = wfc[...]
    second[:, wfc.shape[1] :] = wproj[...]


def open_second_body(size, *refs):
    pieces, (grad, wf, wp, da, cot) = refs[:size], refs[size:]
    chunk = pieces[-1].shape[0]
    cols = wf.shape[1]
    own = cot.shape[0] // 4
    for step, piece in enumerate(pieces):
        place = pl.ds(row_start(lax.axis_index("fsdp"), step, chunk) if size > 1 else 0, chunk)
        wf[place, :] = piece[:, :cols]
        wp[place, :] = piece[:, cols:]
    for block in range(4):
        start = pl.multiple_of((core_place() ^ block) * own, own)
        cot[block * own : (block + 1) * own, :] = grad[pl.ds(start, own), :]
    da[...] = dot(cot[...], wp[...], 1, 0)


def prepare_body(tok0, tok1, tok2, tok3, doc_col, doc_row, pos_col, pos_row, scaled, mask):
    part = tok0.shape[0]
    for number, source in enumerate((tok0, tok1, tok2, tok3)):
        here = slice(number * part, (number + 1) * part)
        scaled[here, :] = norm_parts(source[...].astype(F32))[0]
        seen = (doc_col[here, :] == doc_row[...]) & (pos_row[...] <= pos_col[here, :])
        mask[here, :] = jnp.where(seen, 0.0, -1e30)


def core_place():
    return lax.axis_index("seq") * 2 + lax.axis_index("tensor")


def halves(place, rows):
    half = rows // 2
    first = pl.multiple_of(lax.div(place, 2) * half, half)
    return pl.ds(first, half), pl.ds(pl.multiple_of(half - first, half), half)


def softmax(scores):
    top = jnp.max(scores, axis=-1, keepdims=True)
    raised = jnp.exp(scores - top)
    total = jnp.sum(raised, axis=-1, keepdims=True)
    return (raised * (1.0 / total)).astype(LOW), top + jnp.log(total)


def attend_body(size, *refs):
    pieces, refs = refs[:size], refs[size:]
    sel, scaled, mask = refs[:3]
    qkv, mixed, lse, wqkv, wo, rows, opened, normed, arrived = refs[3:]
    chunk = pieces[0].shape[0]
    split = VEC_COLS + wqkv.shape[1]
    end = split + wo.shape[1]
    copies = []
    for step, piece in enumerate(pieces):
        place = pl.ds(row_start(lax.axis_index("fsdp"), step, chunk) if size > 1 else 0, chunk)
        copies.append(pltpu.make_async_copy(piece, opened.at[place, :], arrived.at[step]))
        copies[-1].start()
    for copy in copies:
        copy.wait()
    wqkv[...] = opened[:, VEC_COLS:split]
    wo[...] = opened[:, split:end]
    wide = opened[:, :VEC_COLS].astype(F32).T
    rows[...] = wide[:8]
    spread = dot(wide[:16].astype(LOW), sel[...], 1, 0)
    col = lax.broadcasted_iota(jnp.int32, (1, qkv.shape[1]), 1)
    count = wo.shape[1]
    bias = jnp.where(col < count, spread[7:8], jnp.where(col >= 2 * count, spread[8:9], 0.0))
    total = qkv.shape[0]
    normed[...] = (scaled[...] * wide[2:3] + wide[3:4]).astype(LOW)
    qkv[...] = (dot(normed[...], wqkv[...], 1, 0) + bias).astype(LOW)
    width = qkv.shape[1] // 3
    heads = width // HEAD_DIM
    half = total // 2
    found_low, found_high = [], []
    low, high = halves(core_place(), total)
    for head in range(heads):
        at = head * HEAD_DIM
        query_low, key_low, value_low = [qkv[low, n * width + at : n * width + at + HEAD_DIM] for n in range(3)]
        query_high, key_high, value_high = [qkv[high, n * width + at : n * width + at + HEAD_DIM] for n in range(3)]
        probs, norm = softmax(dot(query_low, key_low, 1, 1) * 0.125 + mask[:half, :half])
        lse[:half, head : head + 1] = norm
        found_low.append(dot(probs, value_low, 1, 0))
        scores = jnp.concatenate([dot(query_high, key_low, 1, 1), dot(query_high, key_high, 1, 1)], axis=1)
        probs, norm = softmax(scores * 0.125 + mask[half:, :])
        lse[half:, head : head + 1] = norm
        found_high.append(dot(probs[:, :half], value_low, 1, 0) + dot(probs[:, half:], value_high, 1, 0))
    mixed[low, :] = jnp.concatenate(found_low, axis=1).astype(LOW)
    mixed[high, :] = jnp.concatenate(found_high, axis=1).astype(LOW)


def feed_body(
    tok0, tok1, tok2, tok3, mixed0, mixed1, mixed2, mixed3, wo0, wo1, wo2, wo3, wf, rows, da,
    keep, send, middle, normed, active, grad_hidden,
):
    part = tok0.shape[0]
    half = 2 * part
    toks = (tok0, tok1, tok2, tok3)
    for number in range(2):
        here = slice(number * half, (number + 1) * half)
        source = jnp.concatenate([toks[2 * number][...], toks[2 * number + 1][...]], axis=0)
        total = source.astype(F32) + rows[0:1, :]
        for peer, (found, weight) in enumerate(((mixed0, wo0), (mixed1, wo1), (mixed2, wo2), (mixed3, wo3))):
            blocks = [found[(b ^ peer) * part : (b ^ peer) * part + part, :] for b in (2 * number, 2 * number + 1)]
            total += dot(jnp.concatenate(blocks, axis=0), weight[...], 1, 1)
        if number == 0:
            middle[...] = total
        scaled, _ = norm_parts(total)
        low_norm = (scaled * rows[4:5, :] + rows[5:6, :]).astype(LOW)
        normed[here, :] = low_norm
        hidden = dot(low_norm, wf[...], 1, 0) + rows[6:7, :]
        square = hidden * hidden
        bent = jnp.tanh(GELU_SCALE * hidden * (1.0 + 0.044715 * square))
        rise = 0.5 * (1.0 + bent)
        active[here, :] = (hidden * rise).astype(LOW)
        slope = rise + 0.5 * hidden * (1.0 - bent * bent) * (
            GELU_SCALE * (1.0 + 3 * 0.044715 * square)
        )
        grad_low = (da[here, :] * slope).astype(LOW)
        grad_hidden[here, :] = grad_low
        back = dot(grad_low, wf[...], 1, 1)
        if number == 0:
            keep[...] = back
        else:
            send[...] = back.astype(LOW)


def put_pieces(me, outs, parts):
    chunk = outs[0].shape[0]
    for step, out in enumerate(outs):
        place = pl.ds(row_start(me, step, chunk), chunk) if len(outs) > 1 else slice(None)
        low = 0
        for part in parts:
            high = low + part.shape[1]
            out[:, low:high] = part[place, :].astype(out.dtype)
            low = high


def piece_shapes(parts, width, cols):
    return [shape(width // parts, cols, LOW if step else F32) for step in range(parts)]


def feed_grad_body(active, wp, normed, grad_hidden, cot, *refs):
    keep, send, fc_sum = refs[:3]
    pieces, whole = refs[3:-1], refs[-1]
    half = keep.shape[0]
    cols = wp.shape[1]
    whole[:, :cols] = dot(normed[...], grad_hidden[...], 0, 0)
    whole[:, cols:] = dot(cot[...], active[...], 0, 0)
    put_pieces(lax.axis_index("fsdp"), pieces, [whole])
    keep[...] = dot(active[:half, :], wp[...], 1, 1)
    send[...] = dot(active[half:, :], wp[...], 1, 1).astype(LOW)
    fc_sum[...] = jnp.sum(grad_hidden[...].astype(F32), axis=0, keepdims=True)


def middle_body(part_two, far, middle, cot, rows, grad_low, grad_own, early):
    own = grad_own.shape[0]
    flipped = jnp.concatenate([far[own:, :], far[:own, :]], axis=0).astype(F32)
    grad = part_two[...] + flipped
    scaled, inverse = norm_parts(middle[...])
    cotangent = cot[: 2 * own, :].astype(F32)
    total = cotangent + norm_back(grad, scaled, inverse, rows[4:5, :])
    grad_low[...] = total.astype(LOW)
    grad_own[...] = total[:own]
    add = functools.partial(jnp.sum, axis=0, keepdims=True)
    empty = jnp.zeros((2, total.shape[1]), F32)
    early[...] = jnp.concatenate(
        [add(total[:own]), add(cotangent[:own]), empty, add(grad[:own] * scaled[:own]), add(grad[:own]), empty],
        axis=0,
    )


def attend_back_body(
    grad_half, grad_other, wo, wqkv, qkv, lse, scaled, mask, early,
    keep, send, grad_qkv, late, qkv_sum, grad_attn,
):
    total = qkv.shape[0]
    half = total // 2
    width = qkv.shape[1] // 3
    heads = width // HEAD_DIM
    grad_attn[:half, :] = dot(grad_half[...], wo[...], 1, 0).astype(LOW)
    grad_attn[half:, :] = dot(grad_other[...], wo[...], 1, 0).astype(LOW)
    low, high = halves(core_place(), total)
    found_low, found_high = [[], [], []], [[], [], []]
    for head in range(heads):
        at = head * HEAD_DIM
        query_low, key_low, value_low = [qkv[low, n * width + at : n * width + at + HEAD_DIM] for n in range(3)]
        query_high, key_high, value_high = [qkv[high, n * width + at : n * width + at + HEAD_DIM] for n in range(3)]
        grad_low, grad_high = grad_attn[low, at : at + HEAD_DIM], grad_attn[high, at : at + HEAD_DIM]
        scores = dot(query_low, key_low, 1, 1) * 0.125 + mask[:half, :half]
        probs = jnp.exp(scores - lse[:half, head : head + 1])
        grad_probs = dot(grad_low, value_low, 1, 1)
        inner = jnp.sum(probs * grad_probs, axis=-1, keepdims=True)
        first = (probs * (grad_probs - inner)).astype(LOW)
        first_probs = probs.astype(LOW)
        scores = jnp.concatenate([dot(query_high, key_low, 1, 1), dot(query_high, key_high, 1, 1)], axis=1)
        probs = jnp.exp(scores * 0.125 + mask[half:, :] - lse[half:, head : head + 1])
        grad_probs = jnp.concatenate([dot(grad_high, value_low, 1, 1), dot(grad_high, value_high, 1, 1)], axis=1)
        inner = jnp.sum(probs * grad_probs, axis=-1, keepdims=True)
        second = (probs * (grad_probs - inner)).astype(LOW)
        second_probs = probs.astype(LOW)
        found_low[0].append(dot(first, key_low, 1, 0) * 0.125)
        found_high[0].append((dot(second[:, :half], key_low, 1, 0) + dot(second[:, half:], key_high, 1, 0)) * 0.125)
        found_low[1].append((dot(first, query_low, 0, 0) + dot(second[:, :half], query_high, 0, 0)) * 0.125)
        found_high[1].append(dot(second[:, half:], query_high, 0, 0) * 0.125)
        found_low[2].append(dot(first_probs, grad_low, 0, 0) + dot(second_probs[:, :half], grad_high, 0, 0))
        found_high[2].append(dot(second_probs[:, half:], grad_high, 0, 0))
    grad_qkv[low, :] = jnp.concatenate(sum(found_low, []), axis=1).astype(LOW)
    grad_qkv[high, :] = jnp.concatenate(sum(found_high, []), axis=1).astype(LOW)
    gain_sum = shift_sum = 0.0
    for number in range(2):
        here = slice(number * half, (number + 1) * half)
        back = dot(grad_qkv[here, :], wqkv[...], 1, 1)
        gain_sum += jnp.sum(back * scaled[here, :], axis=0, keepdims=True)
        shift_sum += jnp.sum(back, axis=0, keepdims=True)
        if number == 0:
            keep[...] = back
        else:
            send[...] = back.astype(LOW)
    late[...] = jnp.concatenate([early[:2, :], gain_sum, shift_sum, early[4:, :]], axis=0)
    sums = jnp.sum(grad_qkv[...].astype(F32), axis=0, keepdims=True)
    qkv_sum[...] = jnp.concatenate([sums, jnp.zeros((7, sums.shape[1]), F32)], axis=0)


def last_grad_body(
    grad_half, grad_other, mixed, scaled, rows, grad_qkv, fc_sum, qkv_sum, sel, whole, lines, normed
):
    half = grad_half.shape[0]
    normed[...] = (scaled[...] * rows[2:3, :] + rows[3:4, :]).astype(LOW)
    split = grad_qkv.shape[1]
    whole[:, :split] = dot(normed[...], grad_qkv[...], 0, 0)
    whole[:, split:] = dot(grad_half[...], mixed[:half, :], 0, 0) + dot(grad_other[...], mixed[half:, :], 0, 0)
    count = qkv_sum.shape[1] // 3
    col = lax.broadcasted_iota(jnp.int32, qkv_sum.shape, 1)
    line = lax.broadcasted_iota(jnp.int32, qkv_sum.shape, 0)
    sums = qkv_sum[0:1, :]
    sums = jnp.where((line == 0) & (col < count) | (line == 1) & (col >= 2 * count), sums, 0.0)
    placed = lax.dot_general(
        sums, sel[...].astype(F32), (((1,), (1,)), ((), ())),
        preferred_element_type=F32, precision=lax.Precision.HIGHEST,
    )
    lines[...] = jnp.concatenate([fc_sum[...], placed[:7]], axis=0)


def last_cut_body(whole, late, lines, *refs):
    pieces, cols = refs[:-1], refs[-1]
    line = jnp.concatenate([late[:6, :], lines[:3, :]], axis=0)
    lack = jnp.zeros((VEC_COLS - line.shape[0], line.shape[1]), F32)
    cols[...] = jnp.concatenate([line, lack], axis=0).T
    put_pieces(lax.axis_index("fsdp"), pieces, [cols, whole])


def input_body(keep, far, middle_grad, own, rows, out):
    part = own.shape[0]
    grad = keep[:part, :] + far[...].astype(F32)
    scaled, inverse = norm_parts(own[...].astype(F32))
    out[...] = middle_grad[...] + norm_back(grad, scaled, inverse, rows[2:3, :])


def total_of(*refs):
    total = refs[0][...]
    for ref in refs[1:]:
        total = total + ref[...].astype(F32)
    return total


def sum_feed_body(*refs):
    total = total_of(*refs[:4])
    wfc, wproj = refs[4:]
    cols = wfc.shape[1]
    wfc[...] = total[:, :cols]
    wproj[...] = total[:, cols:]


def sum_last_body(*refs):
    total = total_of(*refs[:4])
    wqkv, wout, qv, *vecs = refs[4:]
    width = wout.shape[0]
    for number in range(3):
        low = VEC_COLS + number * width
        wqkv[number] = total[:, low : low + width]
    wout[...] = turned_wide(total[:, VEC_COLS + 3 * width :])
    turned_vecs = turned_wide(total[:, :VEC_COLS])
    for number, vec in enumerate(vecs):
        vec[...] = turned_vecs[number : number + 1]
    qv[...] = turned_vecs[7:9, : qv.shape[1]]


def local(
    tokens,
    segments,
    grad_out,
    w_qkv,
    b_qv,
    w_out,
    b_out,
    w_fc,
    b_fc,
    w_proj,
    b_proj,
    ln1_gain,
    ln1_bias,
    ln2_gain,
    ln2_bias,
):
    size = lax.axis_size("fsdp")
    direct = size == DIRECT_SIZE
    chunk, hidden_cols = w_fc.shape
    own_rows, width = tokens.shape
    seq_rows = segments.shape[0]
    half = 2 * own_rows
    head_cols = w_out.shape[0]
    qkv_cols = 3 * head_cols
    qv_count = b_qv.shape[1]
    parts = size if direct else 1

    near = swap(tokens, "tensor")
    toks = [tokens, near, swap(tokens, "seq"), swap(near, "seq")]

    vecs = [b_out, b_proj, ln1_gain, ln1_bias, ln2_gain, ln2_bias, b_fc]
    col = np.arange(qkv_cols)
    inner = col % head_cols
    source = (inner // qv_count) * chunk + inner % qv_count
    row_number = lax.broadcasted_iota(jnp.int32, (width, qkv_cols), 0)
    sel = (row_number == jnp.asarray(source, jnp.int32)[None, :]).astype(LOW)

    blocks = [lax.axis_index("tensor") ^ b for b in range(4)]
    docs = jnp.concatenate([lax.dynamic_slice_in_dim(segments, b * own_rows, own_rows, 0) for b in blocks])
    spots = jnp.concatenate([b * own_rows + jnp.arange(own_rows, dtype=jnp.int32) for b in blocks])
    marks = [docs[:, None], docs[None, :], spots[:, None], spots[None, :]]
    scaled_one, mask = on_core(
        prepare_body,
        [shape(seq_rows, width, F32), shape(seq_rows, seq_rows, F32)],
        [],
        [*toks, *marks],
    )
    rows_shape = shape(8, width, F32)
    bias_shape = shape(8, qkv_cols, F32)
    if direct:
        (first,) = on_core(
            pack_body,
            [shape(chunk, VEC_COLS + qkv_cols + head_cols, LOW)],
            [],
            [w_qkv, w_out, b_qv, *vecs],
            limit=62,
        )
        (second,) = on_core(pack_second_body, [shape(chunk, 2 * hidden_cols, LOW)], [], [w_fc, w_proj.T])
        firsts = pieces_ring_first(first)
        seconds = pieces_mixed(second, [firsts[6]], mask)
    else:
        lines = jnp.stack([*vecs, *jnp.pad(b_qv, ((0, 0), (0, chunk - qv_count)))])
        lack = jnp.zeros((chunk, VEC_COLS - lines.shape[0]), LOW)
        first = jnp.concatenate([lines.T, lack, w_qkv[0], w_qkv[1], w_qkv[2], w_out.T], axis=1)
        second = jnp.concatenate([w_fc, w_proj.T], axis=1)
        firsts = [lax.all_gather(first, "fsdp", axis=0, tiled=True)]
        seconds = [lax.all_gather(second, "fsdp", axis=0, tiled=True)]
    normed_scratch = pltpu.VMEM((seq_rows, width), LOW)
    qkv, mixed, lse, wqkv, wo, rows = on_core(
        functools.partial(attend_body, parts),
        [
            shape(seq_rows, qkv_cols, LOW),
            shape(seq_rows, head_cols, LOW),
            shape(seq_rows, 128, F32),
            shape(width, qkv_cols, LOW),
            shape(width, head_cols, LOW),
            rows_shape,
        ],
        [],
        [*firsts, sel, scaled_one, mask],
        [
            pltpu.VMEM((width, VEC_COLS + qkv_cols + head_cols), LOW),
            normed_scratch,
            pltpu.SemaphoreType.DMA((parts,)),
        ],
        far=parts,
        flops=2 * seq_rows * (width * qkv_cols + 2 * head_cols * seq_rows),
    )
    wo_near = swap(after(wo, mixed), "tensor")
    wos = [wo, wo_near, swap(wo, "seq"), swap(wo_near, "seq")]
    mixed_near = swap(mixed, "tensor")
    mixeds = [mixed, mixed_near, swap(mixed, "seq"), swap(mixed_near, "seq")]

    square = 2 * seq_rows * width * hidden_cols
    wf, wp, da, cot = on_core(
        functools.partial(open_second_body, parts),
        [
            shape(width, hidden_cols, LOW),
            shape(width, hidden_cols, LOW),
            shape(seq_rows, hidden_cols, F32),
            shape(seq_rows, width, LOW),
        ],
        [],
        [*seconds, grad_out],
        flops=square,
    )
    keep, send, middle, normed_two, active, grad_hidden = on_core(
        feed_body,
        [
            shape(half, width, F32),
            shape(half, width, LOW),
            shape(half, width, F32),
            shape(seq_rows, width, LOW),
            shape(seq_rows, hidden_cols, LOW),
            shape(seq_rows, hidden_cols, LOW),
        ],
        [],
        [*toks, *mixeds, *wos, wf, rows, da],
        flops=3 * square,
    )
    from_core = swap(send, "seq")

    piece_cols = 2 * hidden_cols
    out_keep, out_send, fc_sum, *grad_ff = on_core(
        feed_grad_body,
        [shape(half, width, F32), shape(half, width, LOW), shape(1, hidden_cols, F32), *piece_shapes(parts, width, piece_cols)],
        [],
        [active, wp, normed_two, grad_hidden, cot],
        [pltpu.VMEM((width, piece_cols), F32)],
        flops=3 * square,
    )
    out_half = out_keep + swap(out_send, "seq").astype(F32)
    out_far = swap(out_half[own_rows:].astype(LOW), "tensor")
    result = (middle[:own_rows] + out_half[:own_rows] + out_far.astype(F32) + rows[1:2]).astype(LOW)
    part_two = keep + after(from_core, fc_sum).astype(F32)
    far = swap(part_two.astype(LOW), "tensor")
    if direct:
        begun = sums_begin(grad_ff)
        far = after(far, begun[0], begun[2])
    grad_mid_half, grad_mid_own, early = on_core(
        middle_body,
        [shape(half, width, LOW), shape(own_rows, width, F32), rows_shape],
        [],
        [part_two, far, middle, cot, rows],
    )
    grad_mid_other = swap(grad_mid_half, "seq")

    if direct:
        got_ff = sums_end(grad_ff, begun)
    keep_one, send_one, grad_qkv, late, qkv_sum = on_core(
        attend_back_body,
        [
            shape(half, width, F32),
            shape(half, width, LOW),
            shape(seq_rows, qkv_cols, LOW),
            rows_shape,
            bias_shape,
        ],
        [],
        [grad_mid_half, grad_mid_other, wo, wqkv, qkv, lse, scaled_one, mask, early],
        [pltpu.VMEM((seq_rows, head_cols), LOW)],
        flops=2 * seq_rows * (width * (qkv_cols + head_cols) + 5 * head_cols * seq_rows),
    )
    part_one = keep_one + swap(send_one, "seq").astype(F32)
    far_one = swap(part_one[own_rows:].astype(LOW), "tensor")
    (grad_inputs,) = on_core(
        input_body,
        [shape(own_rows, width, F32)],
        [],
        [part_one, far_one, grad_mid_own, tokens, rows],
    )

    last_cols = VEC_COLS + qkv_cols + head_cols
    whole, lines = on_core(
        last_grad_body,
        [shape(width, qkv_cols + head_cols, F32), rows_shape],
        [],
        [grad_mid_half, grad_mid_other, mixed, scaled_one, rows, grad_qkv, fc_sum, qkv_sum, sel],
        [normed_scratch],
        flops=2 * seq_rows * width * (qkv_cols + head_cols),
    )
    late = late + swap(late, "tensor")
    late = after(late, part_one, lines)
    late = late + swap(late, "seq")
    if direct:
        late = after(late, *begun)
    grad_last = on_core(
        last_cut_body,
        piece_shapes(parts, width, last_cols),
        [],
        [whole, late, lines],
        [pltpu.VMEM((width, VEC_COLS), F32)],
    )

    if direct:
        begun = sums_begin(grad_last)
        begun[1] = after(begun[1], far_one, out_far)
        got_last = sums_end(grad_last, begun)
        grad_wfc, grad_wproj = on_core(
            sum_feed_body,
            [shape(chunk, hidden_cols, F32)] * 2,
            [],
            got_ff,
        )
        grad_wproj = grad_wproj.T
        grad_wqkv, grad_wout, grad_qv, *sums = on_core(
            sum_last_body,
            [jax.ShapeDtypeStruct((3, chunk, head_cols), F32), shape(head_cols, chunk, F32), shape(2, qv_count, F32)]
            + [shape(1, chunk, F32)] * 7,
            [],
            got_last,
        )
    else:
        sum_ff = lax.psum_scatter(grad_ff[0], "fsdp", scatter_dimension=0, tiled=True)
        sum_last = lax.psum_scatter(grad_last[0], "fsdp", scatter_dimension=0, tiled=True)
        grad_wfc, grad_wproj = sum_ff[:, :hidden_cols], sum_ff[:, hidden_cols:].T
        split = VEC_COLS + qkv_cols
        grad_wqkv = sum_last[:, VEC_COLS:split].reshape(chunk, 3, head_cols).transpose(1, 0, 2)
        grad_wout = sum_last[:, split:].T
        sums = sum_last[:, :7].T
        grad_qv = sum_last[:qv_count, 7:9].T

    return (
        result,
        grad_inputs,
        grad_wqkv,
        grad_wout,
        grad_wfc,
        grad_wproj,
        grad_qv,
        *[sums[number].reshape(chunk) for number in (0, 6, 1, 2, 3, 4, 5)],
    )


def solution(mesh):
    in_specs = (
        P(("fsdp", "seq", "tensor"), None),
        P("fsdp"),
        P("fsdp", None),
        P(None, "fsdp", ("seq", "tensor")),
        P(None, ("seq", "tensor", "fsdp")),
        P(("seq", "tensor"), "fsdp"),
        P("fsdp"),
        P("fsdp", ("seq", "tensor")),
        P(("seq", "tensor", "fsdp")),
        P(("seq", "tensor"), "fsdp"),
        P("fsdp"),
        P("fsdp"),
        P("fsdp"),
        P("fsdp"),
        P("fsdp"),
    )
    out_specs = (
        P(("fsdp", "seq", "tensor"), None),
        P(("fsdp", "seq", "tensor"), None),
        P(None, "fsdp", ("seq", "tensor")),
        P(("seq", "tensor"), "fsdp"),
        P("fsdp", ("seq", "tensor")),
        P(("seq", "tensor"), "fsdp"),
        P(None, ("seq", "tensor", "fsdp")),
        P("fsdp"),
        P(("seq", "tensor", "fsdp")),
        P("fsdp"),
        P("fsdp"),
        P("fsdp"),
        P("fsdp"),
        P("fsdp"),
    )
    return jax.shard_map(local, mesh=mesh, in_specs=in_specs, out_specs=out_specs, check_vma=False)
```
